32 devices in a mesh: frame: 8 (over y, x, core), head: 4 (over z).
Axes of the slice: x: 2, y: 2, z: 4, core: 2. Of those that a mesh axis runs over, the one named last changes fastest.
Arguments:
- tokens: bfloat16 [6144, 5120], P('frame', 'head'), may hold values from -40 to 40
- mask_block_frame: int32 [48], replicated, may hold values from 0 to 3, as said below
- attended_key_blocks: int32 [48, 10], replicated, may hold values from 0 to 47, as said below
- frozen_query_key_value: bfloat16 [5120, 3, 3072], P(None, None, 'head'), may hold values from -0.104815686 to 0.104815686
- query_key_value_down_weight: bfloat16 [5120, 192], replicated, may hold values from -0.078125 to 0.078125
- query_key_value_up_weight: bfloat16 [64, 3, 3072], P(None, None, 'head'), may hold values from -0.375 to 0.375
- frozen_output_weight: bfloat16 [3072, 5120], P('head'), may hold values from -0.109375 to 0.109375
- output_down_weight: bfloat16 [3072, 64], P('head'), may hold values from -0.109375 to 0.109375
- output_up_weight: bfloat16 [64, 5120], P(None, 'head'), may hold values from -0.75 to 0.75
Outputs:
- attended_out: bfloat16 [6144, 5120], P('frame', 'head')
The draws below stay inside these ranges and needn't reach their ends.
Inputs may be any that keep to these rules, and one draw needn't show every extreme that they name: `mask_block_frame`: Non-decreasing along the blocks; every frame from 0 to 3 holds at least one block. `attended_key_blocks`: row b lists 10 distinct key blocks and always includes b itself. Take aligned groups of 6 blocks; for a group of query blocks and another group g groups away (g >= 1), the rows of the first group together name exactly 4 // 2 ** (g - 1) distinct blocks of the second, except that a group exactly 4 groups away is named by exactly the larger of that number and 2.
All inputs are finite; a program needn't handle non-finite values.
Results may differ from the reference program's by a relative error of at most 0.017.
Values may be sent and summed in bfloat16 or wider, within the bound.
No kernel may reach another device: no remote copies, remote signals or barrier semaphores. Data moves between devices by JAX's collectives and lax.ppermute only.
A program may use at most 192 MiB of HBM per device.

```python
import math
import jax
import jax.numpy as jnp
from jax import lax

MODEL_WIDTH = 5120
ATTENTION_HEADS = 24
HEAD_SIZE = 128
ADAPTER_RANK = 64
BLOCK = 128
LISTED = 10
PEER_BLOCKS = 4
CLIP_TOKENS = 6144
BLOCKS_DEV = 6
NBLOCKS = 48
FRAMES = 4
N_HEAD = 4


def frame_of_blocks(key):
    cut_key = jax.random.fold_in(key, 11)
    shuffled = jax.random.permutation(cut_key, NBLOCKS - 1) + 1
    cut_points = jnp.sort(shuffled[:FRAMES - 1])
    all_blocks = jnp.arange(NBLOCKS, dtype=jnp.int32)
    return jnp.sum((all_blocks[:, None] >= cut_points[None, :]).astype(jnp.int32), axis=1).astype(jnp.int32)


def draw_mask_block_frame(key, part):
    return frame_of_blocks(key)


def draw_attended_key_blocks(key, part):
    frame_ids = frame_of_blocks(key)
    all_blocks = jnp.arange(NBLOCKS, dtype=jnp.int32)
    same_frame = frame_ids[:, None] == frame_ids[None, :]
    first_block = jnp.min(jnp.where(same_frame, all_blocks[None, :], NBLOCKS), axis=1)
    place = all_blocks - first_block
    groups = NBLOCKS // BLOCKS_DEV
    owner_dev = all_blocks // BLOCKS_DEV
    within = all_blocks % BLOCKS_DEV
    rank_key = jax.random.fold_in(key, 23)
    raw_score = jax.random.randint(rank_key, (groups, groups, BLOCKS_DEV), 0, 4096) * BLOCKS_DEV + jnp.arange(BLOCKS_DEV, dtype=jnp.int32)[None, None, :]
    ordering = jnp.argsort(raw_score, axis=2, stable=True)
    block_rank = jnp.argsort(ordering, axis=2, stable=True).astype(jnp.int32)
    group_ids = jnp.arange(groups, dtype=jnp.int32)
    distance = jnp.abs(group_ids[:, None] - group_ids[None, :])
    near_quota = jnp.where(distance >= 1, PEER_BLOCKS // 2 ** jnp.clip(distance - 1, 0, 20), 0).astype(jnp.int32)
    quota = jnp.where(distance == groups // 2, jnp.maximum(near_quota, PEER_BLOCKS // 2), near_quota).astype(jnp.int32)
    visible = block_rank < quota[:, :, None]
    peer_slot = group_ids[None, :] - (group_ids[None, :] > group_ids[:, None]).astype(jnp.int32)
    order_number = peer_slot[:, :, None] * PEER_BLOCKS + block_rank
    query_owner = owner_dev[:, None]
    key_owner = owner_dev[None, :]
    key_within = within[None, :]
    seen = visible[query_owner, key_owner, key_within]
    needed = seen & (order_number[query_owner, key_owner, key_within] % BLOCKS_DEV == within[:, None])
    allowed = (query_owner == key_owner) | seen
    itself = all_blocks[:, None] == all_blocks[None, :]
    tier = jnp.where(needed | itself, 0, jnp.where(allowed, 1, 2)).astype(jnp.int32)
    frame_gap = jnp.minimum(jnp.abs(frame_ids[:, None] - frame_ids[None, :]), 10)
    spread = (jnp.abs(place[:, None] - place[None, :]) + 1) * 2 ** frame_gap
    jitter = jax.random.randint(jax.random.fold_in(key, 31), (NBLOCKS, NBLOCKS), 0, 4)
    spread = jnp.minimum(spread, 2 ** 14) * 4 + jitter
    score = tier * 2 ** 27 + spread * NBLOCKS + all_blocks[None, :]
    unused, picked = lax.top_k(-score, LISTED)
    return picked.astype(jnp.int32)


def draw_tokens(key, part):
    first_key = jax.random.fold_in(key, 0)
    normal_part = jnp.clip(jax.random.normal(first_key, (CLIP_TOKENS, MODEL_WIDTH), jnp.float32), -6.0, 6.0)
    return normal_part.astype(jnp.bfloat16)


def draw_frozen_query_key_value(key, part):
    first_key = jax.random.fold_in(key, 0)
    shape_full = (MODEL_WIDTH, 3, ATTENTION_HEADS * HEAD_SIZE)
    weights = jnp.clip(jax.random.normal(first_key, shape_full, jnp.float32), -6.0, 6.0) / math.sqrt(MODEL_WIDTH)
    return weights.astype(jnp.bfloat16)


def level_of(stream_key, shape, cuts, low, top_value):
    loudness, own = 1.0, jax.random.fold_in(stream_key, 6)
    for position, blocks in cuts:
        draws = jnp.exp(jax.random.uniform(jax.random.fold_in(own, position), (blocks,), jnp.float32, low / len(cuts), top_value / len(cuts)))
        loudness = loudness * jnp.repeat(draws, shape[position] // blocks).reshape([-1 if axis == position else 1 for axis in range(len(shape))])
    return loudness


def noise(key, shape, deviation, most, cuts=(), kind=jnp.bfloat16):
    entries = deviation * jax.random.normal(key, shape, jnp.float32)
    if cuts:
        entries = entries * level_of(key, shape, cuts, -0.22, 0.18)
    return jnp.clip(entries, -most, most).astype(kind)


def setup_inputs(seed: int = 0) -> dict:
    streams_of = jax.random.split(jax.random.key(seed), 10)
    return {
        "tokens": draw_tokens(jax.random.fold_in(streams_of[9], 71), 0),
        "mask_block_frame": draw_mask_block_frame(jax.random.fold_in(streams_of[9], 71), 0),
        "attended_key_blocks": draw_attended_key_blocks(jax.random.fold_in(streams_of[9], 71), 0),
        "frozen_query_key_value": draw_frozen_query_key_value(jax.random.fold_in(streams_of[9], 71), 0),
        "query_key_value_down_weight": noise(streams_of[4], (MODEL_WIDTH, 3 * ADAPTER_RANK), MODEL_WIDTH ** -0.5, 0.078125),
        "query_key_value_up_weight": noise(streams_of[5], (ADAPTER_RANK, 3, ATTENTION_HEADS * HEAD_SIZE), (4 * ADAPTER_RANK) ** -0.5, 0.375, ((2, 4),)),
        "frozen_output_weight": noise(streams_of[6], (ATTENTION_HEADS * HEAD_SIZE, MODEL_WIDTH), (ATTENTION_HEADS * HEAD_SIZE) ** -0.5, 0.109375, ((0, 4),)),
        "output_down_weight": noise(streams_of[7], (ATTENTION_HEADS * HEAD_SIZE, ADAPTER_RANK), (ATTENTION_HEADS * HEAD_SIZE) ** -0.5, 0.109375, ((0, 4),)),
        "output_up_weight": noise(streams_of[8], (ADAPTER_RANK, MODEL_WIDTH), ADAPTER_RANK ** -0.5, 0.75, ((1, 4),)),
    }


def rotate_pairs(values, frame_pos, place):
    time_pairs = (HEAD_SIZE - 4 * (HEAD_SIZE // 6)) // 2
    space_pairs = (HEAD_SIZE - 2 * time_pairs) // 2
    time_freq = 10000.0 ** (-jnp.arange(time_pairs).astype(jnp.float32) / time_pairs)
    space_freq = 10000.0 ** (-jnp.arange(space_pairs).astype(jnp.float32) / space_pairs)
    time_angle = frame_pos[:, None] * time_freq[None, :]
    space_angle = place[:, None] * space_freq[None, :]
    cos_time = jnp.cos(time_angle)[:, None, :]
    sin_time = jnp.sin(time_angle)[:, None, :]
    cos_space = jnp.cos(space_angle)[:, None, :]
    sin_space = jnp.sin(space_angle)[:, None, :]
    first_part = values[:, :, :time_pairs]
    second_part = values[:, :, time_pairs:2 * time_pairs]
    third_part = values[:, :, 2 * time_pairs:2 * time_pairs + space_pairs]
    fourth_part = values[:, :, 2 * time_pairs + space_pairs:]
    return jnp.concatenate([first_part * cos_time - second_part * sin_time, first_part * sin_time + second_part * cos_time, third_part * cos_space - fourth_part * sin_space, third_part * sin_space + fourth_part * cos_space], axis=-1)

def token_positions(mask_block_frame, block_ids):
    count_blocks = mask_block_frame.shape[0]
    all_blocks = jnp.arange(count_blocks).astype(jnp.int32)
    same_frame = mask_block_frame[:, None] == mask_block_frame[None, :]
    first_block = lax.optimization_barrier(jnp.min(jnp.where(same_frame, all_blocks[None, :], count_blocks), axis=1)).astype(jnp.int32)
    inner_ids = jnp.arange(BLOCK).astype(jnp.int32)
    token_ids = block_ids[:, None] * BLOCK + inner_ids[None, :]
    frame_pos = jnp.broadcast_to(mask_block_frame[block_ids][:, None], token_ids.shape).reshape(-1).astype(jnp.float32)
    place = (token_ids - first_block[block_ids][:, None] * BLOCK).reshape(-1).astype(jnp.float32)
    return (frame_pos, place)

def reference(tokens, mask_block_frame, attended_key_blocks, frozen_query_key_value, query_key_value_down_weight, query_key_value_up_weight, frozen_output_weight, output_down_weight, output_up_weight):
    width = ATTENTION_HEADS * HEAD_SIZE
    adapter_query_key_value = jnp.dot(tokens, query_key_value_down_weight, preferred_element_type=jnp.float32).astype(jnp.bfloat16)
    adapter_query_key_value = lax.optimization_barrier(adapter_query_key_value)
    projected_rows = jnp.dot(tokens, frozen_query_key_value.reshape(MODEL_WIDTH, 3 * width), preferred_element_type=jnp.float32).reshape(CLIP_TOKENS, 3, width)
    projected_rows = projected_rows + jnp.einsum('ngc,cgz->ngz', adapter_query_key_value.reshape(CLIP_TOKENS, 3, ADAPTER_RANK).astype(jnp.float32), query_key_value_up_weight.astype(jnp.float32))
    frame_pos, place = token_positions(mask_block_frame, jnp.arange(NBLOCKS).astype(jnp.int32))
    queries = rotate_pairs(projected_rows[:, 0].reshape(CLIP_TOKENS, ATTENTION_HEADS, HEAD_SIZE), frame_pos, place).astype(jnp.bfloat16)
    keys = rotate_pairs(projected_rows[:, 1].reshape(CLIP_TOKENS, ATTENTION_HEADS, HEAD_SIZE), frame_pos, place).astype(jnp.bfloat16)
    values = projected_rows[:, 2].reshape(CLIP_TOKENS, ATTENTION_HEADS, HEAD_SIZE).astype(jnp.bfloat16)
    query_tiles = queries.reshape(NBLOCKS, BLOCK, ATTENTION_HEADS, HEAD_SIZE)
    key_tiles = keys.reshape(NBLOCKS, BLOCK, ATTENTION_HEADS, HEAD_SIZE)
    value_tiles = values.reshape(NBLOCKS, BLOCK, ATTENTION_HEADS, HEAD_SIZE)

    def attend_block(inputs):
        query_tile, chosen = inputs
        key_rows = key_tiles[chosen].reshape(LISTED * BLOCK, ATTENTION_HEADS, HEAD_SIZE).astype(jnp.float32)
        value_rows = value_tiles[chosen].reshape(LISTED * BLOCK, ATTENTION_HEADS, HEAD_SIZE).astype(jnp.float32)
        scores = jnp.einsum('qhd,khd->hqk', query_tile.astype(jnp.float32), key_rows) / math.sqrt(HEAD_SIZE)
        row_max = lax.optimization_barrier(jnp.max(scores, axis=-1, keepdims=True))
        powers = jnp.exp(scores - row_max)
        probs = (powers / lax.optimization_barrier(jnp.sum(powers, axis=-1, keepdims=True))).astype(jnp.bfloat16)
        probs = lax.optimization_barrier(probs)
        return jnp.einsum('hqk,khd->qhd', probs.astype(jnp.float32), value_rows).astype(jnp.bfloat16)
    attention_result = lax.map(attend_block, (query_tiles, attended_key_blocks)).reshape(CLIP_TOKENS, width)
    adapter_output = jnp.dot(attention_result, output_down_weight, preferred_element_type=jnp.float32).astype(jnp.bfloat16)
    group_width = width // N_HEAD

    def add_group(totals, group):
        columns = lax.dynamic_slice_in_dim(attention_result, group * group_width, group_width, 1)
        weight_rows = lax.dynamic_slice_in_dim(frozen_output_weight, group * group_width, group_width, 0)
        partial_value = jnp.dot(columns, weight_rows, preferred_element_type=jnp.float32).astype(jnp.bfloat16)
        partial_value = lax.optimization_barrier(partial_value)
        return (totals + partial_value.astype(jnp.float32), None)
    frozen_output, unused = lax.scan(add_group, jnp.zeros((CLIP_TOKENS, MODEL_WIDTH), jnp.float32), jnp.arange(N_HEAD).astype(jnp.int32))
    return (frozen_output + jnp.dot(adapter_output, output_up_weight, preferred_element_type=jnp.float32)).astype(jnp.bfloat16)
```

```python
import functools
import math

import jax
import jax.numpy as jnp
from jax import lax
from jax.experimental import pallas as pl
from jax.experimental.pallas import tpu as pltpu
from jax.sharding import PartitionSpec as P

HEAD_SIZE = 128
BLOCK = 128
BF16 = jnp.bfloat16
F32 = jnp.float32
VMEM_LIMIT = 56 * 1024 * 1024
NT = (((1,), (1,)), ((), ()))


def rope_tables(mask_block_frame, first_id, blocks_here):
    time_pairs = (HEAD_SIZE - 4 * (HEAD_SIZE // 6)) // 2
    space_pairs = (HEAD_SIZE - 2 * time_pairs) // 2
    time_freq = 10000.0 ** (-jnp.arange(time_pairs).astype(F32) / time_pairs)
    space_freq = 10000.0 ** (-jnp.arange(space_pairs).astype(F32) / space_pairs)
    count_blocks = mask_block_frame.shape[0]
    all_blocks = jnp.arange(count_blocks, dtype=jnp.int32)
    mine = lax.dynamic_slice_in_dim(mask_block_frame, first_id, blocks_here, 0)
    same_frame = mine[:, None] == mask_block_frame[None, :]
    first_block = jnp.min(jnp.where(same_frame, all_blocks[None, :], count_blocks), axis=1)
    block_ids = first_id + jnp.arange(blocks_here, dtype=jnp.int32)
    token_ids = block_ids[:, None] * BLOCK + jnp.arange(BLOCK, dtype=jnp.int32)[None, :]
    place = (token_ids - first_block[:, None] * BLOCK).reshape(-1).astype(F32)
    frame_pos = jnp.repeat(mine, BLOCK).astype(F32)
    time_angle = frame_pos[:, None] * time_freq[None, :]
    space_angle = place[:, None] * space_freq[None, :]
    ct, st = jnp.cos(time_angle), jnp.sin(time_angle)
    cs, ss = jnp.cos(space_angle), jnp.sin(space_angle)
    zt, zs = jnp.zeros_like(st), jnp.zeros_like(ss)
    cat = lambda *parts: jnp.concatenate(parts, axis=1)
    return jnp.stack(
        [
            cat(ct, ct, cs, cs),
            cat(-st, zt, zs, zs),
            cat(zt, st, zs, zs),
            cat(zt, zt, -ss, zs),
            cat(zt, zt, zs, ss),
        ]
    )


def order_of(offsets, place, n, most):
    source = place - jnp.array(offsets, jnp.int32)
    valid = (source >= 0) & (source < n)
    rank = jnp.cumsum(valid.astype(jnp.int32)) - 1
    count = jnp.sum(valid.astype(jnp.int32))
    index = jnp.minimum(jnp.arange(most, dtype=jnp.int32), jnp.maximum(count - 1, 0))
    hit = valid[None, :] & (rank[None, :] == index[:, None])
    planes = jnp.sum(jnp.where(hit, source[None, :], 0), axis=1)
    return jnp.concatenate([planes, count[None], place[None]]).astype(jnp.int32)


def rotate(u, table_ref):
    time_pairs = (HEAD_SIZE - 4 * (HEAD_SIZE // 6)) // 2
    space_pairs = (HEAD_SIZE - 2 * time_pairs) // 2
    return (
        u * table_ref[0]
        + pltpu.roll(u, HEAD_SIZE - time_pairs, 1) * table_ref[1]
        + pltpu.roll(u, time_pairs, 1) * table_ref[2]
        + pltpu.roll(u, HEAD_SIZE - space_pairs, 1) * table_ref[3]
        + pltpu.roll(u, space_pairs, 1) * table_ref[4]
    )


def project_kernel(n, offsets, pieces, most, groups, chained, final, plan_ref, *refs):
    sections = [section for group in groups for section in group]
    refs = list(refs)
    bufs = [[refs.pop(0) for _ in offsets] for _ in pieces]
    w_ref, down_ref = refs.pop(0), refs.pop(0)
    if chained:
        accin_ref, lowin_ref = refs.pop(0), refs.pop(0)
    if final:
        up_ref, table_ref = refs.pop(0), refs.pop(0)
        out_refs = [refs.pop(0) for _ in groups]
        rank = up_ref.shape[1]
    else:
        acc_ref, lowout_ref = refs.pop(0), refs.pop(0)
    xs, wbuf, dbuf = refs.pop(0), refs.pop(0), refs.pop(0)
    if final:
        acc, low = refs.pop(0), refs.pop(0)
    if chained:
        accin = refs.pop(0)
    xsem, wsem, dsem, asem = refs
    width, depth = xs.shape[2], wbuf.shape[0]
    place = plan_ref[most + 1]
    every = len(offsets) == 2 * n - 1

    def when(k):
        return (lambda f: f()) if every else pl.when(k < plan_ref[most])

    steps = [(i, section, k) for i, section in enumerate(sections) for k in range(most)]

    def weight(index):
        _, section, k = steps[index]
        rows = pl.ds(pl.multiple_of(plan_ref[k] * width, HEAD_SIZE), width)
        return pltpu.make_async_copy(
            w_ref.at[section, rows, :], wbuf.at[index % depth], wsem.at[index % depth]
        )

    def small(k):
        cols = pl.ds(pl.multiple_of(plan_ref[k] * width, HEAD_SIZE), width)
        return pltpu.make_async_copy(down_ref.at[:, cols], dbuf.at[k], dsem.at[k])

    def sums(i):
        return pltpu.make_async_copy(accin_ref.at[sections[i]], accin.at[i], asem.at[i])

    def inputs(act):
        for p, (first, rows) in enumerate(pieces):
            for i, offset in enumerate(offsets):
                source = place - offset

                def go(p=p, first=first, rows=rows, i=i, source=source):
                    dst = xs.at[source, pl.ds(first, rows), :]
                    getattr(pltpu.make_async_copy(bufs[p][i], dst, xsem.at[p, i]), act)()

                go() if offset == 0 else pl.when((source >= 0) & (source < n))(go)

    inputs("start")
    for k in range(most):
        when(k)(lambda k=k: small(k).start())
    for index in range(min(depth, len(steps))):
        when(steps[index][2])(lambda index=index: weight(index).start())
    if chained:
        for i in range(len(sections)):
            sums(i).start()
    inputs("wait")
    lowsum = lowout_ref if not final else low
    lowsum[...] = lowin_ref[...] if chained else jnp.zeros_like(lowsum)
    for k in range(most):

        @when(k)
        def _(k=k):
            small(k).wait()
            lowsum[...] += lax.dot_general(
                xs[plan_ref[k]], dbuf[k], NT, preferred_element_type=F32
            )

    for index, (i, section, k) in enumerate(steps):
        total = acc if final else acc_ref.at[i]
        if k == 0:
            if chained:
                sums(i).wait()
                total[...] = accin[i]
            elif not every and most == 1:
                total[...] = jnp.zeros_like(total)

        @when(k)
        def _(index=index, k=k, total=total):
            weight(index).wait()
            product = jnp.dot(
                xs[plan_ref[k]], wbuf[index % depth], preferred_element_type=F32
            )
            if k == 0 and not chained:
                total[...] = product
            else:
                total[...] += product

        if index + depth < len(steps):
            when(k)(lambda index=index: weight(index + depth).start())
        if final and k == most - 1:
            at = [(g, j) for g, group in enumerate(groups) for j, x in enumerate(group) if x == section]
            out = out_refs[at[0][0]].at[at[0][1]]
            coords = low[:, section * rank : (section + 1) * rank].astype(BF16)
            total[...] += jnp.dot(coords, up_ref[section], preferred_element_type=F32)
            for first in range(0, total.shape[1], HEAD_SIZE):
                head = slice(first, first + HEAD_SIZE)
                u = total[:, head]
                out[:, head] = (u if section == 2 else rotate(u, table_ref)).astype(BF16)


def project(n, place, offsets, most, bufs, w3, down_t, up3=None, tables=None, groups=((0, 1, 2),), sums=None):
    width = bufs[0][0].shape[1]
    pieces, rows = [], 0
    for piece in bufs:
        pieces.append((rows, piece[0].shape[0]))
        rows += piece[0].shape[0]
    local = w3.shape[2]
    coords = down_t.shape[0]
    final, chained = up3 is not None, sums is not None
    count = sum(len(group) for group in groups)
    depth = max(most, count) if most == 1 else most
    any_spec = pl.BlockSpec(memory_space=pl.ANY)
    vmem = pl.BlockSpec(memory_space=pltpu.VMEM)
    operands = [buf for piece in bufs for buf in piece] + [w3, down_t]
    specs = [any_spec] * len(operands)
    if chained:
        operands += list(sums)
        specs += [any_spec, vmem]
    if final:
        operands += [up3, tables]
        specs += [vmem, vmem]
    scratch = [
        pltpu.VMEM((n, rows, width), BF16),
        pltpu.VMEM((depth, width, local), BF16),
        pltpu.VMEM((most, coords, width), BF16),
    ]
    if final:
        scratch += [pltpu.VMEM((rows, local), F32), pltpu.VMEM((rows, coords), F32)]
        shapes = [jax.ShapeDtypeStruct((len(group), rows, local), BF16) for group in groups]
    else:
        shapes = [
            jax.ShapeDtypeStruct((count, rows, local), F32),
            jax.ShapeDtypeStruct((rows, coords), F32),
        ]
    if chained:
        scratch.append(pltpu.VMEM((count, rows, local), F32))
    planes = min(most, n)
    return pl.pallas_call(
        functools.partial(
            project_kernel, n, offsets, tuple(pieces), most, groups, chained, final
        ),
        in_specs=[pl.BlockSpec(memory_space=pltpu.SMEM)] + specs,
        out_specs=[vmem] * len(shapes),
        scratch_shapes=scratch
        + [
            pltpu.SemaphoreType.DMA((len(pieces), len(offsets))),
            pltpu.SemaphoreType.DMA((depth,)),
            pltpu.SemaphoreType.DMA((most,)),
            pltpu.SemaphoreType.DMA((count,)),
        ],
        out_shape=shapes,
        compiler_params=pltpu.CompilerParams(vmem_limit_bytes=VMEM_LIMIT),
        cost_estimate=pl.CostEstimate(
            flops=2 * rows * width * planes * local * count,
            bytes_accessed=2 * width * planes * local * count + 4 * rows * local * count,
            transcendentals=0,
        ),
        name="project_" + ("last" if chained else "all" if final else "most"),
    )(order_of(offsets, place, n, most), *operands)


def attend_kernel(layout, cols, blocks_here, listed, frame_ref, lists_ref, needed_ref, *refs):
    kv = refs[:-7]
    q_ref, out_ref, pool_k, pool_v, keys, values, sems = refs[-7:]
    b = pl.program_id(0)
    width = cols[1] - cols[0]

    @pl.when(b == 0)
    def _():
        for act in ("start", "wait"):
            for mask, i, base, first, count in layout:
                for r in range(count):
                    block = (frame_ref[0] ^ mask) * blocks_here + first + r

                    @pl.when(needed_ref[block] > 0)
                    def _(i=i, base=base, r=r, block=block):
                        for part, pool in ((0, pool_k), (1, pool_v)):
                            copy = pltpu.make_async_copy(
                                kv[i].at[part, pl.ds((base + r) * BLOCK, BLOCK), pl.ds(cols[0], width)],
                                pool.at[block],
                                sems.at[part, block],
                            )
                            getattr(copy, act)()

    for i in range(listed):
        block = lists_ref[b * listed + i]
        keys[i * BLOCK : (i + 1) * BLOCK, :] = pool_k[block]
        values[i * BLOCK : (i + 1) * BLOCK, :] = pool_v[block]
    factor = math.log2(math.e) / math.sqrt(HEAD_SIZE)
    for i in range(width // HEAD_SIZE):
        at = slice(i * HEAD_SIZE, (i + 1) * HEAD_SIZE)
        scores = lax.dot_general(q_ref[:, at], keys[:, at], NT, preferred_element_type=F32)
        top = jnp.max(scores, axis=-1, keepdims=True)
        powers = jnp.exp2((scores - top) * factor)
        total = jnp.sum(powers, axis=-1, keepdims=True)
        mixed = jnp.dot(powers.astype(BF16), values[:, at], preferred_element_type=F32)
        out_ref[:, at] = (mixed / total).astype(BF16)


def attend(frame, lists, needed, layout, kv, q, cols):
    blocks_here, listed = lists.shape
    rows = q.shape[0]
    width = cols[1] - cols[0]
    total = needed.shape[0]
    any_spec = pl.BlockSpec(memory_space=pl.ANY)
    heads = width // HEAD_SIZE
    return pl.pallas_call(
        functools.partial(attend_kernel, layout, cols, blocks_here, listed),
        grid_spec=pltpu.PrefetchScalarGridSpec(
            num_scalar_prefetch=3,
            grid=(blocks_here,),
            in_specs=[any_spec] * len(kv)
            + [pl.BlockSpec((BLOCK, width), lambda b, *_: (b, 0))],
            out_specs=pl.BlockSpec((BLOCK, width), lambda b, *_: (b, 0)),
            scratch_shapes=[
                pltpu.VMEM((total, BLOCK, width), BF16),
                pltpu.VMEM((total, BLOCK, width), BF16),
                pltpu.VMEM((listed * BLOCK, width), BF16),
                pltpu.VMEM((listed * BLOCK, width), BF16),
                pltpu.SemaphoreType.DMA((2, total)),
            ],
        ),
        out_shape=jax.ShapeDtypeStruct((rows, width), BF16),
        compiler_params=pltpu.CompilerParams(vmem_limit_bytes=VMEM_LIMIT),
        cost_estimate=pl.CostEstimate(
            flops=4 * rows * listed * BLOCK * width,
            bytes_accessed=4 * total * BLOCK * width,
            transcendentals=rows * listed * BLOCK * heads,
        ),
        name=f"attend_{cols[0]}",
    )(frame, lists.reshape(-1), needed, *kv, q[:, cols[0] : cols[1]])


def column_tile(width):
    return 2 * HEAD_SIZE if width % (2 * HEAD_SIZE) == 0 else HEAD_SIZE


def spans(parts, members, n):
    out = {}
    for d in range(n):
        taken = [parts[j] for j in sorted(members.get(d, ()))]
        if taken:
            out[d] = (taken[0][0], taken[-1][1])
    return out


def out_kernel(n, members, parts, chained, place_ref, *refs):
    slots = [(j, o) for d, js in members.items() for j in js for o in ((d,) if d == 0 else (d, -d))]
    ranges = spans(parts, members, n)
    bufs = refs[: len(slots)]
    if chained:
        (wother_ref, accin_ref, lowin_ref, up_ref, out_ref, full, weights, low, acc_ref, sems, wsems) = refs[len(slots) :]
    else:
        wown_ref, wother_ref, out_ref, low, full, weights, sems, wsems = refs[len(slots) :]
    place = place_ref[0]
    tile = out_ref.shape[1]
    width = tile * pl.num_programs(0)
    g = pl.program_id(0)

    def at_planes(act):
        for d, (first, last) in ranges.items():
            for o in (d,) if d == 0 else (d, -d):
                source = place - o

                @pl.when((source >= 0) & (source < n))
                def _(d=d, o=o, source=source, first=first, last=last):
                    act(d, o, source, first, last)

    @pl.when(g == 0)
    def _():
        def weight_copy(act):
            def go(d, o, source, first, last):
                rows = pl.ds(first, last - first)
                origin = wown_ref if o == 0 else wother_ref.at[lax.rem(o + n, n) - 1]
                dst = weights.at[source, rows]
                getattr(pltpu.make_async_copy(origin.at[rows], dst, wsems.at[o + n]), act)()

            return go

        def input_copies(act):
            for i, (j, o) in enumerate(slots):
                source = place - o

                @pl.when((source >= 0) & (source < n))
                def _(i=i, j=j, source=source):
                    dst = full.at[source, :, pl.ds(parts[j][0], parts[j][1] - parts[j][0])]
                    getattr(pltpu.make_async_copy(bufs[i], dst, sems.at[i]), act)()

        at_planes(weight_copy("start"))
        input_copies("start")
        at_planes(weight_copy("wait"))
        input_copies("wait")
        low[...] = lowin_ref[...] if chained else jnp.zeros_like(low)

        def coords(d, o, source, first, last):
            low[...] += jnp.dot(
                full[source, :, first:last],
                weights[source, first:last, width:],
                preferred_element_type=F32,
            )

        at_planes(coords)

    at = pl.multiple_of(g * tile, HEAD_SIZE)
    cols = pl.ds(at, tile)
    if chained:
        rank = up_ref.shape[0]
        acc_ref[...] = accin_ref[...] + jnp.dot(
            low[:, :rank].astype(BF16), up_ref[...], preferred_element_type=F32
        )
    else:
        acc_ref = out_ref
        first, last = ranges[0]
        acc_ref[...] = jnp.dot(
            full[place, :, first:last],
            weights[place, first:last, cols],
            preferred_element_type=F32,
        )

    def add(d, o, source, first, last):
        if d:
            acc_ref[...] += jnp.dot(
                full[source, :, first:last],
                weights[source, first:last, cols],
                preferred_element_type=F32,
            )

    at_planes(add)
    if chained:
        out_ref[...] = acc_ref[...].astype(BF16)


def project_out(n, place, members, parts, gathered, weights, width, acc=None, low=None, up=None):
    slots = [(j, o) for d, js in members.items() for j in js for o in ((d,) if d == 0 else (d, -d))]
    bufs = [gathered[j][o] for j, o in slots]
    rows = bufs[0].shape[0]
    local, wide = weights[0].shape[-2:]
    tile = column_tile(width)
    any_spec = pl.BlockSpec(memory_space=pl.ANY)
    tiled = pl.BlockSpec((rows, tile), lambda g, p: (0, g))
    narrow = pl.BlockSpec((rows, wide - width), lambda g, p: (0, 0))
    chained = acc is not None
    scratch = [
        pltpu.VMEM((n, rows, local), BF16),
        pltpu.VMEM((n, local, wide), BF16),
    ]
    if chained:
        scratch += [pltpu.VMEM((rows, wide - width), F32), pltpu.VMEM((rows, tile), F32)]
    flops = sum(
        2 * rows * width * (last - first) for first, last in spans(parts, members, n).values()
    )
    return pl.pallas_call(
        functools.partial(out_kernel, n, members, parts, chained),
        grid_spec=pltpu.PrefetchScalarGridSpec(
            num_scalar_prefetch=1,
            grid=(width // tile,),
            in_specs=[any_spec] * (len(bufs) + len(weights))
            + ([tiled, narrow, pl.BlockSpec((up.shape[0], tile), lambda g, p: (0, g))] if chained else []),
            out_specs=tiled if chained else [tiled, narrow],
            scratch_shapes=scratch
            + [pltpu.SemaphoreType.DMA((len(bufs),)), pltpu.SemaphoreType.DMA((2 * n,))],
        ),
        out_shape=jax.ShapeDtypeStruct((rows, width), BF16)
        if chained
        else [
            jax.ShapeDtypeStruct((rows, width), F32),
            jax.ShapeDtypeStruct((rows, wide - width), F32),
        ],
        compiler_params=pltpu.CompilerParams(vmem_limit_bytes=VMEM_LIMIT),
        cost_estimate=pl.CostEstimate(
            flops=flops, bytes_accessed=6 * rows * width + 2 * local * width, transcendentals=0
        ),
        name="out_last" if chained else "out_most",
    )(place.reshape(1), *bufs, *weights, *((acc, low, up) if chained else ()))


def after(value, *tokens):
    return lax.optimization_barrier((value, tokens))[0] if tokens else value


def step_up(value, axis, n, s):
    return lax.ppermute(value, axis, [(i, i + 1) for i in range(s - 1, n - 1)])


def step_down(value, axis, n, s):
    return lax.ppermute(value, axis, [(i + 1, i) for i in range(n - s)])


def swap(value, size, flip):
    return lax.ppermute(value, "frame", [(i, i ^ flip(i)) for i in range(size)])


def upper_masks(size):
    return sorted(range(2, size, 2), key=lambda m: (bin(m).count("1"), m))


def relay(have, size, mask, *tokens):
    bits = [1 << b for b in range(1, size.bit_length()) if mask >> b & 1]
    a, b = bits[0], bits[-1]
    odd = lax.axis_index("frame") % 2
    sent = after(jnp.where(odd == 0, have[mask ^ b], have[mask ^ a]), *tokens)
    return swap(sent, size, lambda i: a if i % 2 else b)


def chunk_sizes(blocks):
    sizes, left = [], blocks
    while left:
        take = max(1, (left + 1) // 2) if len(sizes) < 2 else left
        sizes.append(take)
        left -= take
    return sizes


def body(
    n,
    frames,
    tokens,
    mask_block_frame,
    attended_key_blocks,
    frozen_query_key_value,
    query_key_value_down_weight,
    query_key_value_up_weight,
    frozen_output_weight,
    output_down_weight,
    output_up_weight,
):
    tok_rows, width = tokens.shape
    blocks_here = tok_rows // BLOCK
    local = frozen_output_weight.shape[0]
    rank = output_up_weight.shape[0]
    frame, place = lax.axis_index("frame"), lax.axis_index("head").astype(jnp.int32)
    frame_s = frame.astype(jnp.int32).reshape(1)
    w3 = frozen_query_key_value.transpose(1, 0, 2)
    up3 = query_key_value_up_weight.transpose(1, 0, 2)
    down_t = query_key_value_down_weight.T
    tables = rope_tables(mask_block_frame, frame * blocks_here, blocks_here)
    lists = lax.dynamic_slice_in_dim(attended_key_blocks, frame * blocks_here, blocks_here, 0)
    count_blocks = attended_key_blocks.shape[0]
    needed = jnp.any(
        lists.reshape(-1)[:, None] == jnp.arange(count_blocks, dtype=jnp.int32)[None, :], axis=0
    ).astype(jnp.int32)
    early = (0,) + tuple(o for s in range(1, n - 1) for o in (s, -s))
    late = (n - 1, 1 - n) if n > 1 else ()
    both = early + late
    uppers = upper_masks(frames)
    single = [m for m in uppers if bin(m).count("1") == 1]
    relayed = [m for m in uppers if bin(m).count("1") > 1]

    line = []

    def step(up, down, s, *tokens_s):
        tokens_s = tokens_s + (line[-2] if len(line) > 1 else ())
        up = lax.ppermute(after(up, *tokens_s), "head", [(i, i + 1) for i in range(s - 1, n - 1)])
        down = lax.ppermute(after(down, *tokens_s), "head", [(i + 1, i) for i in range(n - s)])
        line.append((up, down))
        return up, down

    sizes = chunk_sizes(blocks_here)
    starts = [sum(sizes[:c]) for c in range(len(sizes))]
    slots = []
    for c, size in enumerate(sizes):
        cuts = [size - size // 2, size // 2] if c == 0 else [size]
        at = starts[c] * BLOCK
        slots.append([])
        for cut_size in (x for x in cuts if x):
            slots[c].append({0: tokens[at : at + cut_size * BLOCK]})
            at += cut_size * BLOCK

    def select(c, offsets, *tokens_s):
        chosen = [[bufs[o] for o in offsets] for bufs in slots[c]]
        chosen[0][0] = after(chosen[0][0], *tokens_s)
        return chosen

    steps = [(0, s) for s in range(1, n)]
    rest = [(c, s) for c in range(1, len(sizes)) for s in range(1, n)]
    steps += sorted(rest, key=lambda cs: (cs[1] + 2 * cs[0], -cs[0]))
    layout, pool = [], []
    most, keys_values, queries = {}, {}, {}
    near, far, mine, across = {}, {}, {}, {}

    def project_most(c, *tokens_m):
        if c not in most:
            behind = near.get(c - 1, ()) + mine.get(c - 2, ()) + tokens_m
            most[c] = project(n, place, early, n, select(c, early, *behind), w3, down_t)

    def project_last(c, section, *behind):
        tables_c = tables[:, starts[c] * BLOCK : (starts[c] + sizes[c]) * BLOCK]
        group = (1, 2) if section else (0,)
        return project(
            n, place, late, 1, select(c, late, *behind), w3, down_t, up3, tables_c, (group,), most[c]
        )[0]

    def exchange(c):
        have = {0: after(keys_values[c], *((far[c - 1],) if c else ()))}
        for m in single:
            have[m] = swap(have[0], frames, lambda i: m)
        near[c] = tuple(have[m] for m in single)
        tokens_z = line[-1] if c < len(sizes) - 1 else ()
        if c == len(sizes) - 1:
            for p in range(c + 1):
                if p not in queries:
                    queries[p] = project_last(p, 0, keys_values[c], *((queries[p - 1],) if p else ()))
            tokens_z = mine.get(c - 1, ()) + (queries[c],)
        for m in relayed:
            have[m] = relay(have, frames, m, *tokens_z)
        far[c] = have[relayed[-1]] if relayed else have[0]
        have[0] = keys_values[c]
        for m in [0] + uppers:
            layout.append((m, len(pool), 0, starts[c], sizes[c]))
            pool.append(have[m])
            if frames > 1:
                layout.append((m ^ 1, len(pool), 0, starts[c], sizes[c]))
                pool.append(swap(have[m], frames, lambda i: 1))
                if m in relayed[-1:]:
                    across[c] = (pool[-1],)
                else:
                    mine[c] = mine.get(c, ()) + (pool[-1],)

    def finish(c):
        project_most(c)
        keys_values[c] = project_last(c, 1, *across.get(c - 2, ()))
        exchange(c)

    where = {cs: index for index, cs in enumerate(steps)}
    last = len(sizes) - 1
    bulk_at = {where[c, n - 2] + (3 if c else 2): c for c in range(last) if n > 2}
    ends_at = {where[c, n - 1] + 2: c for c in range(last)}
    for index, (c, s) in enumerate(steps):
        gate = ()
        if index in bulk_at:
            project_most(bulk_at[index], *(line[-2] if bulk_at[index] else ()))
            gate += tuple(most[bulk_at[index]])
        if index in ends_at:
            finish(ends_at[index])
            gate += (keys_values[ends_at[index]],)
            if ends_at[index] == 0:
                queries[0] = project_last(0, 0)
                gate += (queries[0],)
        for bufs in slots[c]:
            bufs[s], bufs[-s] = step(bufs[s - 1], bufs[1 - s], s, *gate)
    for c in range(last):
        if c not in keys_values:
            finish(c)
    finish(last)
    exchanged = near[last]

    extra = -(-rank // HEAD_SIZE) * HEAD_SIZE
    down_pad = jnp.pad(output_down_weight, ((0, 0), (0, extra - rank)))
    rows_each = local // frames

    def columns(weight, down, target):
        return jnp.concatenate([lax.dynamic_slice_in_dim(weight, target * width, width, 1), down], 1)

    wown = columns(frozen_output_weight, down_pad, place)
    cut = lambda value: lax.dynamic_slice_in_dim(value, frame * rows_each, rows_each, 0)
    share, share_down = after((cut(frozen_output_weight), cut(down_pad)), exchanged)
    pieces = []
    for d in range(1, n):
        piece = columns(share, share_down, lax.rem(place + d, n))
        pieces.append(lax.ppermute(piece, "head", [(i, (i + d) % n) for i in range(n)]))
    q = jnp.concatenate([queries[c][0] for c in range(last + 1)], axis=0)
    parts = tuple(
        (start, min(local, start + 2 * HEAD_SIZE)) for start in range(0, local, 2 * HEAD_SIZE)
    )
    gathered = [
        {0: attend(frame_s, lists, needed, tuple(layout), pool, q, cols)} for cols in parts
    ]
    pieces = after(tuple(pieces), gathered[0][0])
    wother = lax.all_gather(jnp.stack(pieces), "frame", axis=1, tiled=True)
    count = len(parts)
    waves = [(j, s) for w in range(1, count + n) for s in range(n - 1, 0, -1) for j in [w - s] if 0 <= j < count]
    waves = sorted(waves, key=lambda js: (js[0] + js[1], js[0]))
    line.clear()
    held = 3
    members = [{0: set(range(count))}, {}]
    for position, (j, s) in enumerate(waves):
        members[0 if position < len(waves) - held - 1 else 1].setdefault(s, set()).add(j)
    members = [{d: tuple(sorted(js)) for d, js in m.items()} for m in members]
    weights = (wown, wother)
    acc = None
    for position, (j, s) in enumerate(waves):
        if position == len(waves) - 1:
            acc, low = project_out(n, place, members[0], parts, gathered, weights, width)
        tokens_s = ()
        if j == 0 and 1 < s <= count:
            tokens_s += (gathered[s - 1][0],)
        up, down = gathered[j][s - 1], gathered[j][1 - s]
        gathered[j][s], gathered[j][-s] = step(up, down, s, *tokens_s)
    return project_out(
        n, place, members[1], parts, gathered, (wother,), width, acc, low, output_up_weight
    )


def solution(mesh):
    return jax.shard_map(
        functools.partial(body, mesh.shape["head"], mesh.shape["frame"]),
        mesh=mesh,
        in_specs=(
            P("frame", "head"),
            P(),
            P(),
            P(None, None, "head"),
            P(),
            P(None, None, "head"),
            P("head", None),
            P("head", None),
            P(None, "head"),
        ),
        out_specs=P("frame", "head"),
        check_vma=False,
    )
```

```python
import functools
import math

import jax
import jax.numpy as jnp
from jax import lax
from jax.experimental import pallas as pl
from jax.experimental.pallas import tpu as pltpu
from jax.sharding import PartitionSpec as P

HEAD_SIZE = 128
BLOCK = 128
BF16 = jnp.bfloat16
F32 = jnp.float32
VMEM_LIMIT = 56 * 1024 * 1024
NT = (((1,), (1,)), ((), ()))


def rope_tables(mask_block_frame, first_id, blocks_here):
    time_pairs = (HEAD_SIZE - 4 * (HEAD_SIZE // 6)) // 2
    space_pairs = (HEAD_SIZE - 2 * time_pairs) // 2
    time_freq = 10000.0 ** (-jnp.arange(time_pairs).astype(F32) / time_pairs)
    space_freq = 10000.0 ** (-jnp.arange(space_pairs).astype(F32) / space_pairs)
    count_blocks = mask_block_frame.shape[0]
    all_blocks = jnp.arange(count_blocks, dtype=jnp.int32)
    mine = lax.dynamic_slice_in_dim(mask_block_frame, first_id, blocks_here, 0)
    same_frame = mine[:, None] == mask_block_frame[None, :]
    first_block = jnp.min(jnp.where(same_frame, all_blocks[None, :], count_blocks), axis=1)
    block_ids = first_id + jnp.arange(blocks_here, dtype=jnp.int32)
    token_ids = block_ids[:, None] * BLOCK + jnp.arange(BLOCK, dtype=jnp.int32)[None, :]
    place = (token_ids - first_block[:, None] * BLOCK).reshape(-1).astype(F32)
    frame_pos = jnp.repeat(mine, BLOCK).astype(F32)
    time_angle = frame_pos[:, None] * time_freq[None, :]
    space_angle = place[:, None] * space_freq[None, :]
    ct, st = jnp.cos(time_angle), jnp.sin(time_angle)
    cs, ss = jnp.cos(space_angle), jnp.sin(space_angle)
    zt, zs = jnp.zeros_like(st), jnp.zeros_like(ss)
    cat = lambda *parts: jnp.concatenate(parts, axis=1)
    return jnp.stack(
        [
            cat(ct, ct, cs, cs),
            cat(-st, zt, zs, zs),
            cat(zt, st, zs, zs),
            cat(zt, zt, -ss, zs),
            cat(zt, zt, zs, ss),
        ]
    )


def order_of(offsets, place, n, most):
    source = place - jnp.array(offsets, jnp.int32)
    valid = (source >= 0) & (source < n)
    rank = jnp.cumsum(valid.astype(jnp.int32)) - 1
    count = jnp.sum(valid.astype(jnp.int32))
    index = jnp.minimum(jnp.arange(most, dtype=jnp.int32), jnp.maximum(count - 1, 0))
    hit = valid[None, :] & (rank[None, :] == index[:, None])
    planes = jnp.sum(jnp.where(hit, source[None, :], 0), axis=1)
    return jnp.concatenate([planes, count[None], place[None]]).astype(jnp.int32)


def rotate(u, table_ref):
    time_pairs = (HEAD_SIZE - 4 * (HEAD_SIZE // 6)) // 2
    space_pairs = (HEAD_SIZE - 2 * time_pairs) // 2
    return (
        u * table_ref[0]
        + pltpu.roll(u, HEAD_SIZE - time_pairs, 1) * table_ref[1]
        + pltpu.roll(u, time_pairs, 1) * table_ref[2]
        + pltpu.roll(u, HEAD_SIZE - space_pairs, 1) * table_ref[3]
        + pltpu.roll(u, space_pairs, 1) * table_ref[4]
    )


def project_kernel(n, offsets, pieces, most, groups, chained, final, start, plan_ref, *refs):
    sections = [section for group in groups for section in group]
    refs = list(refs)
    bufs = [[refs.pop(0) for _ in offsets] for _ in pieces]
    w_ref, down_ref = refs.pop(0), refs.pop(0)
    if chained:
        accin_ref, lowin_ref = refs.pop(0), refs.pop(0)
    if final:
        up_ref, tables_ref = refs.pop(0), refs.pop(0)
        out_refs = [refs.pop(0) for _ in groups]
        rank = up_ref.shape[1]
    else:
        acc_ref, lowout_ref = refs.pop(0), refs.pop(0)
    xs, wbuf, dbuf = refs.pop(0), refs.pop(0), refs.pop(0)
    if final:
        acc, low, table_ref = refs.pop(0), refs.pop(0), refs.pop(0)
    if chained:
        accin = refs.pop(0)
    xsem, wsem, dsem, asem, tsem = refs
    width, depth = xs.shape[2], wbuf.shape[0]
    place = plan_ref[most + 1]
    every = len(offsets) == 2 * n - 1

    def when(k):
        return (lambda f: f()) if every else pl.when(k < plan_ref[most])

    steps = [(i, section, k) for i, section in enumerate(sections) for k in range(most)]

    def weight(index):
        _, section, k = steps[index]
        rows = pl.ds(pl.multiple_of(plan_ref[k] * width, HEAD_SIZE), width)
        return pltpu.make_async_copy(
            w_ref.at[section, rows, :], wbuf.at[index % depth], wsem.at[index % depth]
        )

    def small(k):
        cols = pl.ds(pl.multiple_of(plan_ref[k] * width, HEAD_SIZE), width)
        return pltpu.make_async_copy(down_ref.at[:, cols], dbuf.at[k], dsem.at[k])

    def sums(i):
        return pltpu.make_async_copy(accin_ref.at[sections[i]], accin.at[i], asem.at[i])

    def inputs(act):
        for p, (first, rows) in enumerate(pieces):
            for i, offset in enumerate(offsets):
                source = place - offset

                def go(p=p, first=first, rows=rows, i=i, source=source):
                    dst = xs.at[source, pl.ds(first, rows), :]
                    getattr(pltpu.make_async_copy(bufs[p][i], dst, xsem.at[p, i]), act)()

                go() if offset == 0 else pl.when((source >= 0) & (source < n))(go)

    def angles():
        rows = pl.ds(start, table_ref.shape[1])
        return pltpu.make_async_copy(tables_ref.at[:, rows, :], table_ref, tsem)

    inputs("start")
    if final:
        angles().start()
    for k in range(most):
        when(k)(lambda k=k: small(k).start())
    for index in range(min(depth, len(steps))):
        when(steps[index][2])(lambda index=index: weight(index).start())
    if chained:
        for i in range(len(sections)):
            sums(i).start()
    inputs("wait")
    if final:
        angles().wait()
    lowsum = lowout_ref if not final else low
    lowsum[...] = lowin_ref[...] if chained else jnp.zeros_like(lowsum)
    for k in range(most):

        @when(k)
        def _(k=k):
            small(k).wait()
            lowsum[...] += lax.dot_general(
                xs[plan_ref[k]], dbuf[k], NT, preferred_element_type=F32
            )

    for index, (i, section, k) in enumerate(steps):
        total = acc if final else acc_ref.at[i]
        if k == 0:
            if chained:
                sums(i).wait()
                total[...] = accin[i]
            elif not every and most == 1:
                total[...] = jnp.zeros_like(total)

        @when(k)
        def _(index=index, k=k, total=total):
            weight(index).wait()
            product = jnp.dot(
                xs[plan_ref[k]], wbuf[index % depth], preferred_element_type=F32
            )
            if k == 0 and not chained:
                total[...] = product
            else:
                total[...] += product

        if index + depth < len(steps):
            when(k)(lambda index=index: weight(index + depth).start())
        if final and k == most - 1:
            at = [(g, j) for g, group in enumerate(groups) for j, x in enumerate(group) if x == section]
            out = out_refs[at[0][0]].at[at[0][1]]
            coords = low[:, section * rank : (section + 1) * rank].astype(BF16)
            total[...] += jnp.dot(coords, up_ref[section], preferred_element_type=F32)
            for first in range(0, total.shape[1], HEAD_SIZE):
                head = slice(first, first + HEAD_SIZE)
                u = total[:, head]
                out[:, head] = (u if section == 2 else rotate(u, table_ref)).astype(BF16)


def project(
    n, place, offsets, most, bufs, w3, down_t, up3=None, tables=None, start=0, groups=((0, 1, 2),), sums=None
):
    width = bufs[0][0].shape[1]
    pieces, rows = [], 0
    for piece in bufs:
        pieces.append((rows, piece[0].shape[0]))
        rows += piece[0].shape[0]
    local = w3.shape[2]
    coords = down_t.shape[0]
    final, chained = up3 is not None, sums is not None
    count = sum(len(group) for group in groups)
    depth = max(most, count) if most == 1 else most
    any_spec = pl.BlockSpec(memory_space=pl.ANY)
    vmem = pl.BlockSpec(memory_space=pltpu.VMEM)
    operands = [buf for piece in bufs for buf in piece] + [w3, down_t]
    specs = [any_spec] * len(operands)
    if chained:
        operands += list(sums)
        specs += [any_spec, vmem]
    if final:
        operands += [up3, tables]
        specs += [vmem, any_spec]
    scratch = [
        pltpu.VMEM((n, rows, width), BF16),
        pltpu.VMEM((depth, width, local), BF16),
        pltpu.VMEM((most, coords, width), BF16),
    ]
    if final:
        scratch += [pltpu.VMEM((rows, local), F32), pltpu.VMEM((rows, coords), F32)]
        scratch.append(pltpu.VMEM((tables.shape[0], rows, HEAD_SIZE), F32))
        shapes = [jax.ShapeDtypeStruct((len(group), rows, local), BF16) for group in groups]
    else:
        shapes = [
            jax.ShapeDtypeStruct((count, rows, local), F32),
            jax.ShapeDtypeStruct((rows, coords), F32),
        ]
    if chained:
        scratch.append(pltpu.VMEM((count, rows, local), F32))
    planes = min(most, n)
    return pl.pallas_call(
        functools.partial(
            project_kernel, n, offsets, tuple(pieces), most, groups, chained, final, start
        ),
        in_specs=[pl.BlockSpec(memory_space=pltpu.SMEM)] + specs,
        out_specs=[vmem] * len(shapes),
        scratch_shapes=scratch
        + [
            pltpu.SemaphoreType.DMA((len(pieces), len(offsets))),
            pltpu.SemaphoreType.DMA((depth,)),
            pltpu.SemaphoreType.DMA((most,)),
            pltpu.SemaphoreType.DMA((count,)),
            pltpu.SemaphoreType.DMA,
        ],
        out_shape=shapes,
        compiler_params=pltpu.CompilerParams(vmem_limit_bytes=VMEM_LIMIT),
        cost_estimate=pl.CostEstimate(
            flops=2 * rows * width * planes * local * count,
            bytes_accessed=2 * width * planes * local * count + 4 * rows * local * count,
            transcendentals=0,
        ),
        name="project_" + ("last" if chained else "all" if final else "most"),
    )(order_of(offsets, place, n, most), *operands)


def attend_kernel(layout, cols, blocks_here, listed, per, frame_ref, lists_ref, needed_ref, *refs):
    kv = refs[:-7]
    q_ref, out_ref, pool_k, pool_v, keys, values, sems = refs[-7:]
    b = pl.program_id(0)
    width = cols[1] - cols[0]

    @pl.when(b == 0)
    def _():
        for act in ("start", "wait"):
            for mask, i, base, first, count in layout:
                for r in range(count):
                    block = (frame_ref[0] ^ mask) * blocks_here + first + r

                    @pl.when(needed_ref[block] > 0)
                    def _(i=i, base=base, r=r, block=block):
                        for part, pool in ((0, pool_k), (1, pool_v)):
                            copy = pltpu.make_async_copy(
                                kv[i].at[part, pl.ds((base + r) * BLOCK, BLOCK), pl.ds(cols[0], width)],
                                pool.at[block],
                                sems.at[part, block],
                            )
                            getattr(copy, act)()

    factor = math.log2(math.e) / math.sqrt(HEAD_SIZE)
    heads = width // HEAD_SIZE

    @pl.when(b == 0)
    def _():
        values[...] = jnp.ones_like(values)

    for j in range(per):
        for i in range(listed):
            block = lists_ref[(b * per + j) * listed + i]
            rows = slice(i * BLOCK, (i + 1) * BLOCK)
            keys[j, rows, :] = pool_k[block]
            for h in range(heads):
                values[j, h, rows, :HEAD_SIZE] = pool_v[block, :, h * HEAD_SIZE : (h + 1) * HEAD_SIZE]
    pairs = [(j, h) for j in range(per) for h in range(heads)]
    scores = {}
    for j, h in pairs:
        rows = slice(j * BLOCK, (j + 1) * BLOCK)
        q = q_ref[rows, cols[0] + h * HEAD_SIZE : cols[0] + (h + 1) * HEAD_SIZE]
        scores[j, h] = lax.dot_general(
            q, keys[j, :, h * HEAD_SIZE : (h + 1) * HEAD_SIZE], NT, preferred_element_type=F32
        )
    powers = {}
    for pair in pairs:
        top = jnp.max(scores[pair], axis=-1, keepdims=True)
        powers[pair] = jnp.exp2((scores[pair] - top) * factor).astype(BF16)
    for j, h in pairs:
        mixed = jnp.dot(powers[j, h], values[j, h], preferred_element_type=F32)
        mixed = mixed[:, :HEAD_SIZE] / mixed[:, HEAD_SIZE : HEAD_SIZE + 1]
        out_ref[j * BLOCK : (j + 1) * BLOCK, h * HEAD_SIZE : (h + 1) * HEAD_SIZE] = mixed.astype(BF16)


def attend(frame, lists, needed, layout, kv, q, cols):
    blocks_here, listed = lists.shape
    rows = q.shape[0]
    width = cols[1] - cols[0]
    total = needed.shape[0]
    any_spec = pl.BlockSpec(memory_space=pl.ANY)
    heads = width // HEAD_SIZE
    per = next(p for p in (3, 2, 1) if blocks_here % p == 0)
    return pl.pallas_call(
        functools.partial(attend_kernel, layout, cols, blocks_here, listed, per),
        grid_spec=pltpu.PrefetchScalarGridSpec(
            num_scalar_prefetch=3,
            grid=(blocks_here // per,),
            in_specs=[any_spec] * len(kv)
            + [pl.BlockSpec((per * BLOCK, q.shape[1]), lambda b, *_: (b, 0))],
            out_specs=pl.BlockSpec((per * BLOCK, width), lambda b, *_: (b, 0)),
            scratch_shapes=[
                pltpu.VMEM((total, BLOCK, width), BF16),
                pltpu.VMEM((total, BLOCK, width), BF16),
                pltpu.VMEM((per, listed * BLOCK, width), BF16),
                pltpu.VMEM((per, heads, listed * BLOCK, 2 * HEAD_SIZE), BF16),
                pltpu.SemaphoreType.DMA((2, total)),
            ],
        ),
        out_shape=jax.ShapeDtypeStruct((rows, width), BF16),
        compiler_params=pltpu.CompilerParams(vmem_limit_bytes=VMEM_LIMIT),
        cost_estimate=pl.CostEstimate(
            flops=4 * rows * listed * BLOCK * width,
            bytes_accessed=4 * total * BLOCK * width,
            transcendentals=rows * listed * BLOCK * heads,
        ),
        name=f"attend_{cols[0]}",
    )(frame, lists.reshape(-1), needed, *kv, q)


def column_tile(width):
    return 2 * HEAD_SIZE if width % (2 * HEAD_SIZE) == 0 else HEAD_SIZE


def spans(parts, members, n):
    out = {}
    for d in range(n):
        taken = [parts[j] for j in sorted(members.get(d, ()))]
        if taken:
            out[d] = (taken[0][0], taken[-1][1])
    return out


def out_kernel(n, members, parts, chained, place_ref, *refs):
    slots = [(j, o) for d, js in members.items() for j in js for o in ((d,) if d == 0 else (d, -d))]
    ranges = spans(parts, members, n)
    bufs = refs[: len(slots)]
    if chained:
        (wother_ref, accin_ref, lowin_ref, up_ref, out_ref, full, weights, low, acc_ref, sems, wsems) = refs[len(slots) :]
    else:
        wown_ref, wother_ref, out_ref, low, full, weights, sems, wsems = refs[len(slots) :]
    place = place_ref[0]
    tile = out_ref.shape[1]
    width = tile * pl.num_programs(0)
    g = pl.program_id(0)

    def at_planes(act):
        for d, (first, last) in ranges.items():
            for o in (d,) if d == 0 else (d, -d):
                source = place - o

                @pl.when((source >= 0) & (source < n))
                def _(d=d, o=o, source=source, first=first, last=last):
                    act(d, o, source, first, last)

    @pl.when(g == 0)
    def _():
        def weight_copy(act):
            def go(d, o, source, first, last):
                rows = pl.ds(first, last - first)
                origin = wown_ref if o == 0 else wother_ref.at[lax.rem(o + n, n) - 1]
                dst = weights.at[source, rows]
                getattr(pltpu.make_async_copy(origin.at[rows], dst, wsems.at[o + n]), act)()

            return go

        def input_copies(act):
            for i, (j, o) in enumerate(slots):
                source = place - o

                @pl.when((source >= 0) & (source < n))
                def _(i=i, j=j, source=source):
                    dst = full.at[source, :, pl.ds(parts[j][0], parts[j][1] - parts[j][0])]
                    getattr(pltpu.make_async_copy(bufs[i], dst, sems.at[i]), act)()

        at_planes(weight_copy("start"))
        input_copies("start")
        at_planes(weight_copy("wait"))
        input_copies("wait")
        low[...] = lowin_ref[...] if chained else jnp.zeros_like(low)

        def coords(d, o, source, first, last):
            low[...] += jnp.dot(
                full[source, :, first:last],
                weights[source, first:last, width:],
                preferred_element_type=F32,
            )

        at_planes(coords)

    at = pl.multiple_of(g * tile, HEAD_SIZE)
    cols = pl.ds(at, tile)
    if chained:
        rank = up_ref.shape[0]
        acc_ref[...] = accin_ref[...] + jnp.dot(
            low[:, :rank].astype(BF16), up_ref[...], preferred_element_type=F32
        )
    else:
        acc_ref = out_ref
        first, last = ranges[0]
        acc_ref[...] = jnp.dot(
            full[place, :, first:last],
            weights[place, first:last, cols],
            preferred_element_type=F32,
        )

    def add(d, o, source, first, last):
        if d:
            acc_ref[...] += jnp.dot(
                full[source, :, first:last],
                weights[source, first:last, cols],
                preferred_element_type=F32,
            )

    at_planes(add)
    if chained:
        out_ref[...] = acc_ref[...].astype(BF16)


def project_out(n, place, members, parts, gathered, weights, width, acc=None, low=None, up=None):
    slots = [(j, o) for d, js in members.items() for j in js for o in ((d,) if d == 0 else (d, -d))]
    bufs = [gathered[j][o] for j, o in slots]
    rows = bufs[0].shape[0]
    local, wide = weights[0].shape[-2:]
    tile = column_tile(width)
    any_spec = pl.BlockSpec(memory_space=pl.ANY)
    tiled = pl.BlockSpec((rows, tile), lambda g, p: (0, g))
    narrow = pl.BlockSpec((rows, wide - width), lambda g, p: (0, 0))
    chained = acc is not None
    scratch = [
        pltpu.VMEM((n, rows, local), BF16),
        pltpu.VMEM((n, local, wide), BF16),
    ]
    if chained:
        scratch += [pltpu.VMEM((rows, wide - width), F32), pltpu.VMEM((rows, tile), F32)]
    flops = sum(
        2 * rows * width * (last - first) for first, last in spans(parts, members, n).values()
    )
    return pl.pallas_call(
        functools.partial(out_kernel, n, members, parts, chained),
        grid_spec=pltpu.PrefetchScalarGridSpec(
            num_scalar_prefetch=1,
            grid=(width // tile,),
            in_specs=[any_spec] * (len(bufs) + len(weights))
            + ([tiled, narrow, pl.BlockSpec((up.shape[0], tile), lambda g, p: (0, g))] if chained else []),
            out_specs=tiled if chained else [tiled, narrow],
            scratch_shapes=scratch
            + [pltpu.SemaphoreType.DMA((len(bufs),)), pltpu.SemaphoreType.DMA((2 * n,))],
        ),
        out_shape=jax.ShapeDtypeStruct((rows, width), BF16)
        if chained
        else [
            jax.ShapeDtypeStruct((rows, width), F32),
            jax.ShapeDtypeStruct((rows, wide - width), F32),
        ],
        compiler_params=pltpu.CompilerParams(vmem_limit_bytes=VMEM_LIMIT),
        cost_estimate=pl.CostEstimate(
            flops=flops, bytes_accessed=6 * rows * width + 2 * local * width, transcendentals=0
        ),
        name="out_last" if chained else "out_most",
    )(place.reshape(1), *bufs, *weights, *((acc, low, up) if chained else ()))


def after(value, *tokens):
    return lax.optimization_barrier((value, tokens))[0] if tokens else value


def step_up(value, axis, n, s):
    return lax.ppermute(value, axis, [(i, i + 1) for i in range(s - 1, n - 1)])


def step_down(value, axis, n, s):
    return lax.ppermute(value, axis, [(i + 1, i) for i in range(n - s)])


def swap(value, size, flip):
    return lax.ppermute(value, "frame", [(i, i ^ flip(i)) for i in range(size)])


def upper_masks(size):
    return sorted(range(2, size, 2), key=lambda m: (bin(m).count("1"), m))


def relay(have, size, mask, *tokens):
    bits = [1 << b for b in range(1, size.bit_length()) if mask >> b & 1]
    a, b = bits[0], bits[-1]
    odd = lax.axis_index("frame") % 2
    sent = after(jnp.where(odd == 0, have[mask ^ b], have[mask ^ a]), *tokens)
    return swap(sent, size, lambda i: a if i % 2 else b)


def body(
    n,
    frames,
    tokens,
    mask_block_frame,
    attended_key_blocks,
    frozen_query_key_value,
    query_key_value_down_weight,
    query_key_value_up_weight,
    frozen_output_weight,
    output_down_weight,
    output_up_weight,
):
    tok_rows, width = tokens.shape
    blocks_here = tok_rows // BLOCK
    local = frozen_output_weight.shape[0]
    rank = output_up_weight.shape[0]
    frame, place = lax.axis_index("frame"), lax.axis_index("head").astype(jnp.int32)
    frame_s = frame.astype(jnp.int32).reshape(1)
    w3 = frozen_query_key_value.transpose(1, 0, 2)
    up3 = query_key_value_up_weight.transpose(1, 0, 2)
    down_t = query_key_value_down_weight.T
    tables = rope_tables(mask_block_frame, frame * blocks_here, blocks_here)
    lists = lax.dynamic_slice_in_dim(attended_key_blocks, frame * blocks_here, blocks_here, 0)
    count_blocks = attended_key_blocks.shape[0]
    needed = jnp.any(
        lists.reshape(-1)[:, None] == jnp.arange(count_blocks, dtype=jnp.int32)[None, :], axis=0
    ).astype(jnp.int32)
    early = (0,) + tuple(o for s in range(1, n - 1) for o in (s, -s))
    late = (n - 1, 1 - n) if n > 1 else ()
    both = early + late
    uppers = upper_masks(frames)
    single = [m for m in uppers if bin(m).count("1") == 1]
    relayed = [m for m in uppers if bin(m).count("1") > 1]

    line = []

    def step(up, down, s, *tokens_s):
        tokens_s = tokens_s + (line[-2] if len(line) > 1 else ())
        up = lax.ppermute(after(up, *tokens_s), "head", [(i, i + 1) for i in range(s - 1, n - 1)])
        down = lax.ppermute(after(down, *tokens_s), "head", [(i + 1, i) for i in range(n - s)])
        line.append((up, down))
        return up, down

    cuts = [0, (blocks_here + 1) // 2, blocks_here] if blocks_here > 1 else [0, blocks_here]
    chunks = [(first, last - first) for first, last in zip(cuts, cuts[1:])]
    slots = [{0: tokens[at * BLOCK : (at + size) * BLOCK]} for at, size in chunks]
    most = {}
    soon = tuple(o for o in early if abs(o) <= max(n - 3, 0))
    then = tuple(o for o in early if o not in soon)

    def select(c, offsets, *tokens_s):
        chosen = [slots[c][o] for o in offsets]
        return [[after(chosen[0], *tokens_s)] + chosen[1:]]

    def begin(c):
        if (c, 0) not in most:
            most[c, 0] = project(n, place, soon, min(n, len(soon)), select(c, soon), w3, down_t)
        return tuple(most[c, 0])

    def bulk(c):
        if (c, 1) not in most:
            most[c, 1] = begin(c)
            if then:
                slices = 2 if 2 * (n - 2) <= n - 1 else 1
                most[c, 1] = project(
                    n, place, then, slices, select(c, then), w3, down_t, sums=most[c, 0]
                )
        return tuple(most[c, 1])

    def ends(c, group, *tokens_e):
        start = chunks[c][0] * BLOCK
        bufs = select(c, late, *tokens_e)
        return project(
            n, place, late, 1, bufs, w3, down_t, up3, tables, start, (group,), most[c, 1]
        )[0]

    last = len(chunks) - 1
    for s in range(1, n):
        for c in range(len(chunks)):
            gate = ()
            if s == n - 1 and s > 1:
                gate = begin(0) + begin(last) if c == 0 else bulk(0)
            slots[c][s], slots[c][-s] = step(slots[c][s - 1], slots[c][1 - s], s, *gate)
    settled = bulk(last)

    extra = -(-rank // HEAD_SIZE) * HEAD_SIZE
    down_pad = jnp.pad(output_down_weight, ((0, 0), (0, extra - rank)))
    rows_each = local // frames

    def columns(weight, down, target):
        return jnp.concatenate([lax.dynamic_slice_in_dim(weight, target * width, width, 1), down], 1)

    wown = columns(frozen_output_weight, down_pad, place)
    cut = lambda value: lax.dynamic_slice_in_dim(value, frame * rows_each, rows_each, 0)
    share, share_down = after((cut(frozen_output_weight), cut(down_pad)), *line[-1])
    pieces = []
    for d in range(1, n):
        piece = columns(share, share_down, lax.rem(place + d, n))
        pieces.append(lax.ppermute(piece, "head", [(i, (i + d) % n) for i in range(n)]))
    keys_values, queries, haves = [], [], []
    for c in range(len(chunks)):
        keys_values.append(ends(c, (1, 2), *settled))
        settled = ()
        haves.append({0: keys_values[c]})
        for m in single:
            haves[c][m] = swap(keys_values[c], frames, lambda i: m)
    crossed = [{} for _ in chunks]
    for c in range(len(chunks)):
        queries.append(ends(c, (0,), keys_values[-1], *(queries[-1:] if c else pieces)))
    for c, have in enumerate(haves):
        tokens_z = (keys_values[-1],)
        if c == last:
            tokens_z = (queries[-1],)
            if c and frames > 1:
                tokens_z += tuple(crossed[c - 1][m] for m in [0] + single)
        for m in relayed:
            have[m] = relay(have, frames, m, *tokens_z)
        for m in [0] + uppers:
            if frames > 1:
                crossed[c][m] = swap(have[m], frames, lambda i: 1)
    layout, pool = [], []
    for c, (first, size) in enumerate(chunks):
        for m in [0] + uppers:
            for flip, held in ((0, haves[c]), (1, crossed[c])):
                if m in held:
                    layout.append((m ^ flip, len(pool), 0, first, size))
                    pool.append(held[m])

    q = jnp.concatenate([value[0] for value in queries], axis=0)
    middle = (local // HEAD_SIZE + 1) // 2 * HEAD_SIZE
    parts = ((0, middle), (middle, local)) if middle < local else ((0, local),)
    gathered = []
    for cols in parts:
        earlier = tuple(one[0] for one in gathered[-1:])
        attended = attend(frame_s, lists, needed, tuple(layout), pool, after(q, *earlier), cols)
        gathered.append({0: attended})
    count = len(parts)
    waves = [(j, s) for w in range(1, count + n) for s in range(n - 1, 0, -1) for j in [w - s] if 0 <= j < count]
    waves = sorted(waves, key=lambda js: (js[0] + js[1], js[0]))
    line.clear()
    members = [{0: set(range(count))}, {}]
    for position, (j, s) in enumerate(waves):
        members[0 if position < len(waves) - 2 else 1].setdefault(s, set()).add(j)
    members = [{d: tuple(sorted(js)) for d, js in m.items()} for m in members]
    acc = None
    for position, (j, s) in enumerate(waves):
        if position == 1:
            pieces = after(tuple(pieces), gathered[min(1, count - 1)][0], gathered[0][1], gathered[0][-1])
            wother = lax.all_gather(jnp.stack(pieces), "frame", axis=1, tiled=True)
            weights = (wown, wother)
        if position == len(waves) - 1:
            acc, low = project_out(n, place, members[0], parts, gathered, weights, width)
        tokens_s = ()
        if j == 0 and 1 < s <= count:
            tokens_s += (gathered[s - 1][0],)
        up, down = gathered[j][s - 1], gathered[j][1 - s]
        gathered[j][s], gathered[j][-s] = step(up, down, s, *tokens_s)
    return project_out(
        n, place, members[1], parts, gathered, (wother,), width, acc, low, output_up_weight
    )


def solution(mesh):
    return jax.shard_map(
        functools.partial(body, mesh.shape["head"], mesh.shape["frame"]),
        mesh=mesh,
        in_specs=(
            P("frame", "head"),
            P(),
            P(),
            P(None, None, "head"),
            P(),
            P(None, None, "head"),
            P("head", None),
            P("head", None),
            P(None, "head"),
        ),
        out_specs=P("frame", "head"),
        check_vma=False,
    )
```

```python
import functools
import math

import jax
import jax.numpy as jnp
from jax import lax
from jax.experimental import pallas as pl
from jax.experimental.pallas import tpu as pltpu
from jax.sharding import PartitionSpec as P

HEAD_SIZE = 128
BLOCK = 128
BF16 = jnp.bfloat16
F32 = jnp.float32
VMEM_LIMIT = 56 * 1024 * 1024
NT = (((1,), (1,)), ((), ()))


def rope_tables(mask_block_frame, first_id, blocks_here):
    time_pairs = (HEAD_SIZE - 4 * (HEAD_SIZE // 6)) // 2
    space_pairs = (HEAD_SIZE - 2 * time_pairs) // 2
    time_freq = 10000.0 ** (-jnp.arange(time_pairs).astype(F32) / time_pairs)
    space_freq = 10000.0 ** (-jnp.arange(space_pairs).astype(F32) / space_pairs)
    count_blocks = mask_block_frame.shape[0]
    all_blocks = jnp.arange(count_blocks, dtype=jnp.int32)
    mine = lax.dynamic_slice_in_dim(mask_block_frame, first_id, blocks_here, 0)
    same_frame = mine[:, None] == mask_block_frame[None, :]
    first_block = jnp.min(jnp.where(same_frame, all_blocks[None, :], count_blocks), axis=1)
    block_ids = first_id + jnp.arange(blocks_here, dtype=jnp.int32)
    token_ids = block_ids[:, None] * BLOCK + jnp.arange(BLOCK, dtype=jnp.int32)[None, :]
    place = (token_ids - first_block[:, None] * BLOCK).reshape(-1).astype(F32)
    frame_pos = jnp.repeat(mine, BLOCK).astype(F32)
    time_angle = frame_pos[:, None] * time_freq[None, :]
    space_angle = place[:, None] * space_freq[None, :]
    ct, st = jnp.cos(time_angle), jnp.sin(time_angle)
    cs, ss = jnp.cos(space_angle), jnp.sin(space_angle)
    zt, zs = jnp.zeros_like(st), jnp.zeros_like(ss)
    cat = lambda *parts: jnp.concatenate(parts, axis=1)
    return jnp.stack(
        [
            cat(ct, ct, cs, cs),
            cat(-st, zt, zs, zs),
            cat(zt, st, zs, zs),
            cat(zt, zt, -ss, zs),
            cat(zt, zt, zs, ss),
        ]
    )


def order_of(offsets, place, n, most):
    source = place - jnp.array(offsets, jnp.int32)
    valid = (source >= 0) & (source < n)
    rank = jnp.cumsum(valid.astype(jnp.int32)) - 1
    count = jnp.sum(valid.astype(jnp.int32))
    index = jnp.minimum(jnp.arange(most, dtype=jnp.int32), jnp.maximum(count - 1, 0))
    hit = valid[None, :] & (rank[None, :] == index[:, None])
    planes = jnp.sum(jnp.where(hit, source[None, :], 0), axis=1)
    return jnp.concatenate([planes, count[None], place[None]]).astype(jnp.int32)


def rotate(u, table_ref):
    time_pairs = (HEAD_SIZE - 4 * (HEAD_SIZE // 6)) // 2
    space_pairs = (HEAD_SIZE - 2 * time_pairs) // 2
    return (
        u * table_ref[0]
        + pltpu.roll(u, HEAD_SIZE - time_pairs, 1) * table_ref[1]
        + pltpu.roll(u, time_pairs, 1) * table_ref[2]
        + pltpu.roll(u, HEAD_SIZE - space_pairs, 1) * table_ref[3]
        + pltpu.roll(u, space_pairs, 1) * table_ref[4]
    )


def project_kernel(n, offsets, pieces, most, groups, chained, final, start, plan_ref, *refs):
    sections = [section for group in groups for section in group]
    refs = list(refs)
    bufs = [[refs.pop(0) for _ in offsets] for _ in pieces]
    w_ref, down_ref = refs.pop(0), refs.pop(0)
    if chained:
        accin_ref, lowin_ref = refs.pop(0), refs.pop(0)
    if final:
        up_ref, tables_ref = refs.pop(0), refs.pop(0)
        out_refs = [refs.pop(0) for _ in groups]
        rank = up_ref.shape[1]
    else:
        acc_ref, lowout_ref = refs.pop(0), refs.pop(0)
    xs, wbuf, dbuf = refs.pop(0), refs.pop(0), refs.pop(0)
    if final:
        acc, low, table_ref = refs.pop(0), refs.pop(0), refs.pop(0)
    if chained:
        accin = refs.pop(0)
    xsem, wsem, dsem, asem, tsem = refs
    width, depth = xs.shape[2], wbuf.shape[0]
    place = plan_ref[most + 1]
    every = len(offsets) == 2 * n - 1

    def when(k):
        return (lambda f: f()) if every else pl.when(k < plan_ref[most])

    steps = [(i, section, k) for i, section in enumerate(sections) for k in range(most)]

    def weight(index):
        _, section, k = steps[index]
        rows = pl.ds(pl.multiple_of(plan_ref[k] * width, HEAD_SIZE), width)
        return pltpu.make_async_copy(
            w_ref.at[section, rows, :], wbuf.at[index % depth], wsem.at[index % depth]
        )

    def small(k):
        cols = pl.ds(pl.multiple_of(plan_ref[k] * width, HEAD_SIZE), width)
        return pltpu.make_async_copy(down_ref.at[:, cols], dbuf.at[k], dsem.at[k])

    def sums(i):
        return pltpu.make_async_copy(accin_ref.at[sections[i]], accin.at[i], asem.at[i])

    def inputs(act):
        for p, (first, rows) in enumerate(pieces):
            for i, offset in enumerate(offsets):
                source = place - offset

                def go(p=p, first=first, rows=rows, i=i, source=source):
                    dst = xs.at[source, pl.ds(first, rows), :]
                    getattr(pltpu.make_async_copy(bufs[p][i], dst, xsem.at[p, i]), act)()

                go() if offset == 0 else pl.when((source >= 0) & (source < n))(go)

    def angles():
        rows = pl.ds(start, table_ref.shape[1])
        return pltpu.make_async_copy(tables_ref.at[:, rows, :], table_ref, tsem)

    inputs("start")
    if final:
        angles().start()
    for k in range(most):
        when(k)(lambda k=k: small(k).start())
    for index in range(min(depth, len(steps))):
        when(steps[index][2])(lambda index=index: weight(index).start())
    if chained:
        for i in range(len(sections)):
            sums(i).start()
    inputs("wait")
    if final:
        angles().wait()
    lowsum = lowout_ref if not final else low
    lowsum[...] = lowin_ref[...] if chained else jnp.zeros_like(lowsum)
    for k in range(most):

        @when(k)
        def _(k=k):
            small(k).wait()
            lowsum[...] += lax.dot_general(
                xs[plan_ref[k]], dbuf[k], NT, preferred_element_type=F32
            )

    for index, (i, section, k) in enumerate(steps):
        total = acc if final else acc_ref.at[i]
        if k == 0:
            if chained:
                sums(i).wait()
                total[...] = accin[i]
            elif not every and most == 1:
                total[...] = jnp.zeros_like(total)

        @when(k)
        def _(index=index, k=k, total=total):
            weight(index).wait()
            product = jnp.dot(
                xs[plan_ref[k]], wbuf[index % depth], preferred_element_type=F32
            )
            if k == 0 and not chained:
                total[...] = product
            else:
                total[...] += product

        if index + depth < len(steps):
            when(k)(lambda index=index: weight(index + depth).start())
        if final and k == most - 1:
            at = [(g, j) for g, group in enumerate(groups) for j, x in enumerate(group) if x == section]
            out = out_refs[at[0][0]].at[at[0][1]]
            coords = low[:, section * rank : (section + 1) * rank].astype(BF16)
            total[...] += jnp.dot(coords, up_ref[section], preferred_element_type=F32)
            for first in range(0, total.shape[1], HEAD_SIZE):
                head = slice(first, first + HEAD_SIZE)
                u = total[:, head]
                out[:, head] = (u if section == 2 else rotate(u, table_ref)).astype(BF16)


def project(
    n, place, offsets, most, bufs, w3, down_t, up3=None, tables=None, start=0, groups=((0, 1, 2),), sums=None
):
    width = bufs[0][0].shape[1]
    pieces, rows = [], 0
    for piece in bufs:
        pieces.append((rows, piece[0].shape[0]))
        rows += piece[0].shape[0]
    local = w3.shape[2]
    coords = down_t.shape[0]
    final, chained = up3 is not None, sums is not None
    count = sum(len(group) for group in groups)
    depth = max(most, count) if most == 1 else most
    any_spec = pl.BlockSpec(memory_space=pl.ANY)
    vmem = pl.BlockSpec(memory_space=pltpu.VMEM)
    operands = [buf for piece in bufs for buf in piece] + [w3, down_t]
    specs = [any_spec] * len(operands)
    if chained:
        operands += list(sums)
        specs += [any_spec, vmem]
    if final:
        operands += [up3, tables]
        specs += [vmem, any_spec]
    scratch = [
        pltpu.VMEM((n, rows, width), BF16),
        pltpu.VMEM((depth, width, local), BF16),
        pltpu.VMEM((most, coords, width), BF16),
    ]
    if final:
        scratch += [pltpu.VMEM((rows, local), F32), pltpu.VMEM((rows, coords), F32)]
        scratch.append(pltpu.VMEM((tables.shape[0], rows, HEAD_SIZE), F32))
        shapes = [jax.ShapeDtypeStruct((len(group), rows, local), BF16) for group in groups]
    else:
        shapes = [
            jax.ShapeDtypeStruct((count, rows, local), F32),
            jax.ShapeDtypeStruct((rows, coords), F32),
        ]
    if chained:
        scratch.append(pltpu.VMEM((count, rows, local), F32))
    planes = min(most, n)
    return pl.pallas_call(
        functools.partial(
            project_kernel, n, offsets, tuple(pieces), most, groups, chained, final, start
        ),
        in_specs=[pl.BlockSpec(memory_space=pltpu.SMEM)] + specs,
        out_specs=[vmem] * len(shapes),
        scratch_shapes=scratch
        + [
            pltpu.SemaphoreType.DMA((len(pieces), len(offsets))),
            pltpu.SemaphoreType.DMA((depth,)),
            pltpu.SemaphoreType.DMA((most,)),
            pltpu.SemaphoreType.DMA((count,)),
            pltpu.SemaphoreType.DMA,
        ],
        out_shape=shapes,
        compiler_params=pltpu.CompilerParams(vmem_limit_bytes=VMEM_LIMIT),
        cost_estimate=pl.CostEstimate(
            flops=2 * rows * width * planes * local * count,
            bytes_accessed=2 * width * planes * local * count + 4 * rows * local * count,
            transcendentals=0,
        ),
        name="project_" + ("last" if chained else "all" if final else "most"),
    )(order_of(offsets, place, n, most), *operands)


def attend_kernel(layout, cols, chunks, listed, per, frame_ref, lists_ref, needed_ref, *refs):
    kv, q_refs = refs[: -8 - chunks], refs[-8 - chunks : -8]
    out_ref, pool_k, pool_v, keys, values, q_all, sems, qsems = refs[-8:]
    b = pl.program_id(0)
    width = cols[1] - cols[0]

    @pl.when(b == 0)
    def _():
        for act in ("start", "wait"):
            at = 0
            for c, piece in enumerate(q_refs):
                rows = piece.shape[1]
                dst = q_all.at[pl.ds(at, rows), :]
                source = piece.at[0, :, pl.ds(cols[0], width)]
                getattr(pltpu.make_async_copy(source, dst, qsems.at[c]), act)()
                at += rows
            blocks_here = at // BLOCK
            for mask, i, base, first, count in layout:
                for r in range(count):
                    block = (frame_ref[0] ^ mask) * blocks_here + first + r

                    @pl.when(needed_ref[block] > 0)
                    def _(i=i, base=base, r=r, block=block):
                        for part, pool in ((0, pool_k), (1, pool_v)):
                            copy = pltpu.make_async_copy(
                                kv[i].at[part, pl.ds((base + r) * BLOCK, BLOCK), pl.ds(cols[0], width)],
                                pool.at[block],
                                sems.at[part, block],
                            )
                            getattr(copy, act)()

    factor = math.log2(math.e) / math.sqrt(HEAD_SIZE)
    heads = width // HEAD_SIZE

    @pl.when(b == 0)
    def _():
        values[...] = jnp.ones_like(values)

    for j in range(per):
        for i in range(listed):
            block = lists_ref[(b * per + j) * listed + i]
            rows = slice(i * BLOCK, (i + 1) * BLOCK)
            keys[j, rows, :] = pool_k[block]
            for h in range(heads):
                values[j, h, rows, :HEAD_SIZE] = pool_v[block, :, h * HEAD_SIZE : (h + 1) * HEAD_SIZE]
    pairs = [(j, h) for j in range(per) for h in range(heads)]
    scores = {}
    for j, h in pairs:
        rows = pl.ds(pl.multiple_of((b * per + j) * BLOCK, BLOCK), BLOCK)
        q = q_all[rows, h * HEAD_SIZE : (h + 1) * HEAD_SIZE]
        scores[j, h] = lax.dot_general(
            q, keys[j, :, h * HEAD_SIZE : (h + 1) * HEAD_SIZE], NT, preferred_element_type=F32
        )
    powers = {}
    for pair in pairs:
        top = jnp.max(scores[pair], axis=-1, keepdims=True)
        powers[pair] = jnp.exp2((scores[pair] - top) * factor).astype(BF16)
    for j, h in pairs:
        mixed = jnp.dot(powers[j, h], values[j, h], preferred_element_type=F32)
        mixed = mixed[:, :HEAD_SIZE] / mixed[:, HEAD_SIZE : HEAD_SIZE + 1]
        out_ref[j * BLOCK : (j + 1) * BLOCK, h * HEAD_SIZE : (h + 1) * HEAD_SIZE] = mixed.astype(BF16)


def attend(frame, lists, needed, layout, kv, queries, cols):
    blocks_here, listed = lists.shape
    rows = blocks_here * BLOCK
    width = cols[1] - cols[0]
    total = needed.shape[0]
    any_spec = pl.BlockSpec(memory_space=pl.ANY)
    heads = width // HEAD_SIZE
    per = next(p for p in (3, 2, 1) if blocks_here % p == 0)
    return pl.pallas_call(
        functools.partial(attend_kernel, layout, cols, len(queries), listed, per),
        grid_spec=pltpu.PrefetchScalarGridSpec(
            num_scalar_prefetch=3,
            grid=(blocks_here // per,),
            in_specs=[any_spec] * (len(kv) + len(queries)),
            out_specs=pl.BlockSpec((per * BLOCK, width), lambda b, *_: (b, 0)),
            scratch_shapes=[
                pltpu.VMEM((total, BLOCK, width), BF16),
                pltpu.VMEM((total, BLOCK, width), BF16),
                pltpu.VMEM((per, listed * BLOCK, width), BF16),
                pltpu.VMEM((per, heads, listed * BLOCK, 2 * HEAD_SIZE), BF16),
                pltpu.VMEM((rows, width), BF16),
                pltpu.SemaphoreType.DMA((2, total)),
                pltpu.SemaphoreType.DMA((len(queries),)),
            ],
        ),
        out_shape=jax.ShapeDtypeStruct((rows, width), BF16),
        compiler_params=pltpu.CompilerParams(vmem_limit_bytes=VMEM_LIMIT),
        cost_estimate=pl.CostEstimate(
            flops=4 * rows * listed * BLOCK * width,
            bytes_accessed=4 * total * BLOCK * width,
            transcendentals=rows * listed * BLOCK * heads,
        ),
        name=f"attend_{cols[0]}",
    )(frame, lists.reshape(-1), needed, *kv, *queries)


def column_tile(width):
    return 2 * HEAD_SIZE if width % (2 * HEAD_SIZE) == 0 else HEAD_SIZE


def spans(parts, members, n):
    out = {}
    for d in range(n):
        taken = [parts[j] for j in sorted(members.get(d, ()))]
        if taken:
            out[d] = (taken[0][0], taken[-1][1])
    return out


def out_kernel(n, members, parts, chained, place_ref, *refs):
    slots = [(j, o) for d, js in members.items() for j in js for o in ((d,) if d == 0 else (d, -d))]
    ranges = spans(parts, members, n)
    bufs = refs[: len(slots)]
    if chained:
        (wother_ref, accin_ref, lowin_ref, up_ref, out_ref, full, weights, low, acc_ref, sems, wsems) = refs[len(slots) :]
    else:
        wown_ref, wother_ref, out_ref, low, full, weights, sems, wsems = refs[len(slots) :]
    place = place_ref[0]
    tile = out_ref.shape[1]
    width = tile * pl.num_programs(0)
    g = pl.program_id(0)

    def at_planes(act):
        for d, (first, last) in ranges.items():
            for o in (d,) if d == 0 else (d, -d):
                source = place - o

                @pl.when((source >= 0) & (source < n))
                def _(d=d, o=o, source=source, first=first, last=last):
                    act(d, o, source, first, last)

    @pl.when(g == 0)
    def _():
        def weight_copy(act):
            def go(d, o, source, first, last):
                rows = pl.ds(first, last - first)
                origin = wown_ref if o == 0 else wother_ref.at[lax.rem(o + n, n) - 1]
                dst = weights.at[source, rows]
                getattr(pltpu.make_async_copy(origin.at[rows], dst, wsems.at[o + n]), act)()

            return go

        def input_copies(act):
            for i, (j, o) in enumerate(slots):
                source = place - o

                @pl.when((source >= 0) & (source < n))
                def _(i=i, j=j, source=source):
                    dst = full.at[source, :, pl.ds(parts[j][0], parts[j][1] - parts[j][0])]
                    getattr(pltpu.make_async_copy(bufs[i], dst, sems.at[i]), act)()

        at_planes(weight_copy("start"))
        input_copies("start")
        at_planes(weight_copy("wait"))
        input_copies("wait")
        low[...] = lowin_ref[...] if chained else jnp.zeros_like(low)

        def coords(d, o, source, first, last):
            low[...] += jnp.dot(
                full[source, :, first:last],
                weights[source, first:last, width:],
                preferred_element_type=F32,
            )

        at_planes(coords)

    at = pl.multiple_of(g * tile, HEAD_SIZE)
    cols = pl.ds(at, tile)
    if chained:
        rank = up_ref.shape[0]
        acc_ref[...] = accin_ref[...] + jnp.dot(
            low[:, :rank].astype(BF16), up_ref[...], preferred_element_type=F32
        )
    else:
        acc_ref = out_ref
        first, last = ranges[0]
        acc_ref[...] = jnp.dot(
            full[place, :, first:last],
            weights[place, first:last, cols],
            preferred_element_type=F32,
        )

    def add(d, o, source, first, last):
        if d:
            acc_ref[...] += jnp.dot(
                full[source, :, first:last],
                weights[source, first:last, cols],
                preferred_element_type=F32,
            )

    at_planes(add)
    if chained:
        out_ref[...] = acc_ref[...].astype(BF16)


def project_out(n, place, members, parts, gathered, weights, width, acc=None, low=None, up=None):
    slots = [(j, o) for d, js in members.items() for j in js for o in ((d,) if d == 0 else (d, -d))]
    bufs = [gathered[j][o] for j, o in slots]
    rows = bufs[0].shape[0]
    local, wide = weights[0].shape[-2:]
    tile = column_tile(width)
    any_spec = pl.BlockSpec(memory_space=pl.ANY)
    tiled = pl.BlockSpec((rows, tile), lambda g, p: (0, g))
    narrow = pl.BlockSpec((rows, wide - width), lambda g, p: (0, 0))
    chained = acc is not None
    scratch = [
        pltpu.VMEM((n, rows, local), BF16),
        pltpu.VMEM((n, local, wide), BF16),
    ]
    if chained:
        scratch += [pltpu.VMEM((rows, wide - width), F32), pltpu.VMEM((rows, tile), F32)]
    flops = sum(
        2 * rows * width * (last - first) for first, last in spans(parts, members, n).values()
    )
    return pl.pallas_call(
        functools.partial(out_kernel, n, members, parts, chained),
        grid_spec=pltpu.PrefetchScalarGridSpec(
            num_scalar_prefetch=1,
            grid=(width // tile,),
            in_specs=[any_spec] * (len(bufs) + len(weights))
            + ([tiled, narrow, pl.BlockSpec((up.shape[0], tile), lambda g, p: (0, g))] if chained else []),
            out_specs=tiled if chained else [tiled, narrow],
            scratch_shapes=scratch
            + [pltpu.SemaphoreType.DMA((len(bufs),)), pltpu.SemaphoreType.DMA((2 * n,))],
        ),
        out_shape=jax.ShapeDtypeStruct((rows, width), BF16)
        if chained
        else [
            jax.ShapeDtypeStruct((rows, width), F32),
            jax.ShapeDtypeStruct((rows, wide - width), F32),
        ],
        compiler_params=pltpu.CompilerParams(vmem_limit_bytes=VMEM_LIMIT),
        cost_estimate=pl.CostEstimate(
            flops=flops, bytes_accessed=6 * rows * width + 2 * local * width, transcendentals=0
        ),
        name="out_last" if chained else "out_most",
    )(place.reshape(1), *bufs, *weights, *((acc, low, up) if chained else ()))


def after(value, *tokens):
    return lax.optimization_barrier((value, tokens))[0] if tokens else value


def step_up(value, axis, n, s):
    return lax.ppermute(value, axis, [(i, i + 1) for i in range(s - 1, n - 1)])


def step_down(value, axis, n, s):
    return lax.ppermute(value, axis, [(i + 1, i) for i in range(n - s)])


def swap(value, size, flip):
    return lax.ppermute(value, "frame", [(i, i ^ flip(i)) for i in range(size)])


def upper_masks(size):
    return sorted(range(2, size, 2), key=lambda m: (bin(m).count("1"), m))


def relay(have, size, mask, *tokens):
    bits = [1 << b for b in range(1, size.bit_length()) if mask >> b & 1]
    a, b = bits[0], bits[-1]
    odd = lax.axis_index("frame") % 2
    sent = after(jnp.where(odd == 0, have[mask ^ b], have[mask ^ a]), *tokens)
    return swap(sent, size, lambda i: a if i % 2 else b)


def body(
    n,
    frames,
    tokens,
    mask_block_frame,
    attended_key_blocks,
    frozen_query_key_value,
    query_key_value_down_weight,
    query_key_value_up_weight,
    frozen_output_weight,
    output_down_weight,
    output_up_weight,
):
    tok_rows, width = tokens.shape
    blocks_here = tok_rows // BLOCK
    local = frozen_output_weight.shape[0]
    rank = output_up_weight.shape[0]
    frame, place = lax.axis_index("frame"), lax.axis_index("head").astype(jnp.int32)
    frame_s = frame.astype(jnp.int32).reshape(1)
    w3 = frozen_query_key_value.transpose(1, 0, 2)
    up3 = query_key_value_up_weight.transpose(1, 0, 2)
    down_t = query_key_value_down_weight.T
    tables = rope_tables(mask_block_frame, frame * blocks_here, blocks_here)
    lists = lax.dynamic_slice_in_dim(attended_key_blocks, frame * blocks_here, blocks_here, 0)
    count_blocks = attended_key_blocks.shape[0]
    needed = jnp.any(
        lists.reshape(-1)[:, None] == jnp.arange(count_blocks, dtype=jnp.int32)[None, :], axis=0
    ).astype(jnp.int32)
    early = (0,) + tuple(o for s in range(1, n - 1) for o in (s, -s))
    late = (n - 1, 1 - n) if n > 1 else ()
    both = early + late
    uppers = upper_masks(frames)
    single = [m for m in uppers if bin(m).count("1") == 1]
    relayed = [m for m in uppers if bin(m).count("1") > 1]

    line = []

    def step(up, down, s, *tokens_s):
        tokens_s = tokens_s + (line[-2] if len(line) > 1 else ())
        up = lax.ppermute(after(up, *tokens_s), "head", [(i, i + 1) for i in range(s - 1, n - 1)])
        down = lax.ppermute(after(down, *tokens_s), "head", [(i + 1, i) for i in range(n - s)])
        line.append((up, down))
        return up, down

    cuts = [0, (blocks_here + 1) // 2, blocks_here] if blocks_here > 1 else [0, blocks_here]
    chunks = [(first, last - first) for first, last in zip(cuts, cuts[1:])]
    slots = [{0: tokens[at * BLOCK : (at + size) * BLOCK]} for at, size in chunks]
    most = {}
    soon = tuple(o for o in early if abs(o) <= max(n - 3, 0))
    then = tuple(o for o in early if o not in soon)

    def select(c, offsets, *tokens_s):
        chosen = [slots[c][o] for o in offsets]
        return [[after(chosen[0], *tokens_s)] + chosen[1:]]

    def begin(c):
        if (c, 0) not in most:
            most[c, 0] = project(n, place, soon, min(n, len(soon)), select(c, soon), w3, down_t)
        return tuple(most[c, 0])

    def bulk(c):
        if (c, 1) not in most:
            most[c, 1] = begin(c)
            if then:
                slices = 2 if 2 * (n - 2) <= n - 1 else 1
                most[c, 1] = project(
                    n, place, then, slices, select(c, then), w3, down_t, sums=most[c, 0]
                )
        return tuple(most[c, 1])

    def ends(c, group, *tokens_e):
        start = chunks[c][0] * BLOCK
        bufs = select(c, late, *tokens_e)
        return project(
            n, place, late, 1, bufs, w3, down_t, up3, tables, start, (group,), most[c, 1]
        )[0]

    last = len(chunks) - 1
    for s in range(1, n):
        for c in range(len(chunks)):
            gate = ()
            if s == n - 1 and s > 1:
                gate = begin(0) + begin(last) if c == 0 else bulk(0)
            slots[c][s], slots[c][-s] = step(slots[c][s - 1], slots[c][1 - s], s, *gate)
    settled = bulk(last)

    extra = -(-rank // HEAD_SIZE) * HEAD_SIZE
    down_pad = jnp.pad(output_down_weight, ((0, 0), (0, extra - rank)))
    rows_each = local // frames

    def columns(weight, down, target):
        return jnp.concatenate([lax.dynamic_slice_in_dim(weight, target * width, width, 1), down], 1)

    wown = columns(frozen_output_weight, down_pad, place)
    cut = lambda value: lax.dynamic_slice_in_dim(value, frame * rows_each, rows_each, 0)
    share, share_down = after((cut(frozen_output_weight), cut(down_pad)), *line[-1])
    pieces = []
    for d in range(1, n):
        piece = columns(share, share_down, lax.rem(place + d, n))
        pieces.append(lax.ppermute(piece, "head", [(i, (i + d) % n) for i in range(n)]))
    keys_values, queries, haves = [], [], []
    for c in range(len(chunks)):
        keys_values.append(ends(c, (1, 2), *settled))
        settled = ()
        haves.append({0: keys_values[c]})
        for m in single:
            haves[c][m] = swap(keys_values[c], frames, lambda i: m)
    crossed = [{} for _ in chunks]
    for c in range(len(chunks)):
        queries.append(ends(c, (0,), keys_values[-1], *(queries[-1:] if c else pieces)))
    for c, have in enumerate(haves):
        tokens_z = (keys_values[-1],)
        if c == last:
            tokens_z = (queries[-1],)
            if c and frames > 1:
                tokens_z += tuple(crossed[c - 1][m] for m in [0] + single)
        for m in relayed:
            have[m] = relay(have, frames, m, *tokens_z)
        for m in [0] + uppers:
            if frames > 1:
                crossed[c][m] = swap(have[m], frames, lambda i: 1)
    layout, pool = [], []
    for c, (first, size) in enumerate(chunks):
        for m in [0] + uppers:
            for flip, held in ((0, haves[c]), (1, crossed[c])):
                if m in held:
                    layout.append((m ^ flip, len(pool), 0, first, size))
                    pool.append(held[m])

    middle = (local // HEAD_SIZE + 1) // 2 * HEAD_SIZE
    parts = ((0, middle), (middle, local)) if middle < local else ((0, local),)
    gathered = []
    for cols in parts:
        earlier = tuple(one[0] for one in gathered[-1:])
        attended = attend(frame_s, lists, needed, tuple(layout), pool, after(queries, *earlier), cols)
        gathered.append({0: attended})
    count = len(parts)
    inner = ([1, n - 1] + list(range(2, n - 1))) if n > 2 else [1] * (n - 1)
    waves = [(j, s) for j in range(count) for s in inner]
    members = [{0: set(range(count))}, {}]
    for position, (j, s) in enumerate(waves):
        members[0 if position < len(waves) - 1 else 1].setdefault(s, set()).add(j)
    members = [{d: tuple(sorted(js)) for d, js in m.items()} for m in members]
    for j, s in waves:
        held, tokens_s = gathered[j], ()
        if s in (1, n - 1):
            tokens_s = tuple(gathered[j - 1][o] for o in (1, -1, n - 1)) if j else ()
        elif j:
            tokens_s = (held[n - 1], gathered[j - 1][n - 2], gathered[j - 1][2 - n])
        else:
            tokens_s = (held[n - 1], gathered[min(1, count - 1)][0])
        if s == n - 1:
            own = after(held[0], *tokens_s)
            held[s] = held[-s] = lax.ppermute(own, "head", [(0, n - 1), (n - 1, 0)])
        else:
            up, down = after((held[s - 1], held[1 - s]), *tokens_s)
            held[s] = lax.ppermute(up, "head", [(i, i + 1) for i in range(s - 1, n - 1)])
            held[-s] = lax.ppermute(down, "head", [(i + 1, i) for i in range(n - s)])
    started = tuple(gathered[0][o] for o in (1, -1, n - 1)) if n > 1 else ()
    pieces = after(tuple(pieces), gathered[min(1, count - 1)][0], *started)
    wother = lax.all_gather(jnp.stack(pieces), "frame", axis=1, tiled=True)
    acc, low = project_out(n, place, members[0], parts, gathered, (wown, wother), width)
    return project_out(
        n, place, members[1], parts, gathered, (wother,), width, acc, low, output_up_weight
    )


def solution(mesh):
    return jax.shard_map(
        functools.partial(body, mesh.shape["head"], mesh.shape["frame"]),
        mesh=mesh,
        in_specs=(
            P("frame", "head"),
            P(),
            P(),
            P(None, None, "head"),
            P(),
            P(None, None, "head"),
            P("head", None),
            P("head", None),
            P(None, "head"),
        ),
        out_specs=P("frame", "head"),
        check_vma=False,
    )
```
